256 devices in a mesh: ctx: 32 (over x, z_hi, y), exp: 8 (over z_lo, core).
Axes of the slice: x: 4, y: 4, z: 8 (z_hi: 2, z_lo: 4; z = z_hi * 4 + z_lo), core: 2. Of those that a mesh axis runs over, the one named last changes fastest.
Arguments:
- queries: bfloat16 [4096, 6144], P('ctx', 'exp'), may hold values from -8 to 8
- keys: bfloat16 [4096, 1024], P('ctx', 'exp'), may hold values from -8 to 8
- values: bfloat16 [4096, 1024], P('ctx', 'exp'), may hold values from -6 to 6
- span_order: int32 [64], replicated, may hold values from 0 to 63, each once
- norm_gain: bfloat16 [6144], replicated, may hold values from 0.099609375 to 1.8984375
- router_weight: bfloat16 [6144, 8], replicated, may hold values from -0.078125 to 0.078125
- routes: int32 [4096, 2], P(('ctx', 'exp')), may hold values from 0 to 7, all different within a row
- priority: int32 [256, 32], P(('ctx', 'exp')), may hold values from 0 to 31, each once within a row
- w_gate: bfloat16 [8, 6144, 8192], P('exp', None, 'ctx'), may hold values from -0.078125 to 0.078125
- w_up: bfloat16 [8, 6144, 8192], P('exp', None, 'ctx'), may hold values from -0.078125 to 0.078125
- w_down: bfloat16 [8, 8192, 6144], P('exp', 'ctx'), may hold values from -0.0625 to 0.0625
Outputs:
- layer_out: bfloat16 [4096, 6144], P(('ctx', 'exp'))
The draws below stay inside these ranges and needn't reach their ends.
Inputs may be any that keep to these rules, and one draw needn't show every extreme that they name: `routes`: each token names two different experts. `priority`: each row is a permutation of 0 to 31. `span_order`: A permutation of 0 to 63.
All inputs are finite; a program needn't handle non-finite values.
Results may differ from the reference program's by a relative error of at most 0.02.
Values may be sent and summed in bfloat16 or wider, within the bound.
A program may use at most 128 MiB of HBM per device.

```python
from functools import partial
import jax
import jax.numpy as jnp
from jax import lax

D = 6144
HEADS = 48
KV_HEADS = 8
HD = 128
FF = 8192
TOK_DEV = 128
EXPERTS = 8
LEN = 4096
SPAN = 64
ROWS_DEV = 16
BLOCKS = 256
CAP = 4
N_CTX = 32


def draw_queries(key, part):
    key = jax.random.fold_in(key, 11)
    base = jnp.clip(jax.random.normal(key, (LEN, HEADS, HD), jnp.float32), -8.0, 8.0)
    return base.reshape(LEN, D).astype(jnp.bfloat16)


def draw_keys(key, part):
    key = jax.random.fold_in(key, 12)
    base = jnp.clip(jax.random.normal(key, (LEN, KV_HEADS, HD), jnp.float32), -8.0, 8.0)
    return base.reshape(LEN, KV_HEADS * HD).astype(jnp.bfloat16)


def levels(rng, dims, pieces, smallest, top_value):
    def one(position, shards_of):
        draws = jax.random.uniform(jax.random.fold_in(jax.random.fold_in(rng, 6), position), (shards_of,), jnp.float32, smallest / len(pieces), top_value / len(pieces))
        return jnp.repeat(jnp.exp(draws), dims[position] // shards_of).reshape((-1,) + (1,) * (len(dims) - position - 1))

    level = one(*pieces[0])
    for cut in pieces[1:]:
        level = level * one(*cut)
    return level


def different_ones(stream_key, rows, count, top, lift):
    ranking = jax.random.permutation(jax.random.fold_in(stream_key, 1), count)
    pull = ranking
    for power in range(3):
        pull = pull * pull // count
    pull = pull * lift // count
    tickets = jax.random.randint(jax.random.fold_in(stream_key, 2), (rows, count), 0, 4096) + pull
    sure = jax.random.permutation(jax.random.fold_in(stream_key, 3), rows)[jnp.arange(count) % rows]
    tickets = jnp.where(jnp.arange(rows)[:, None] == sure[None, :], 1 << 14, tickets)
    score = tickets * count + jnp.arange(count)
    return lax.top_k(score.astype(jnp.int32), top)[1].astype(jnp.int32)


def normal_values(rng, extent, scale, limit, pieces=(), kind=jnp.bfloat16):
    factor_of = levels(rng, extent, pieces, -0.22, 0.18) if pieces else 1.0
    drawn = jax.random.normal(rng, extent, jnp.float32) * scale * factor_of
    return jnp.minimum(jnp.maximum(drawn, -limit), limit).astype(kind)


def setup_inputs(seed: int = 0) -> dict:
    key_of = jax.random.split(jax.random.key(seed), 12)
    return {
        "queries": draw_queries(jax.random.fold_in(key_of[11], 71), 0),
        "keys": draw_keys(jax.random.fold_in(key_of[11], 71), 0),
        "values": normal_values(key_of[2], (LEN, KV_HEADS * HD), 1.0, 6.0, ((0, 32), (1, 8))),
        "span_order": jax.random.permutation(key_of[3], 2 * N_CTX).astype(jnp.int32),
        "norm_gain": jnp.clip(1.0 + 0.18 * jax.random.normal(key_of[4], (D,), jnp.float32), 0.099609375, 1.8984375).astype(jnp.bfloat16),
        "router_weight": normal_values(key_of[5], (D, EXPERTS), D ** -0.5, 0.078125),
        "routes": different_ones(key_of[6], LEN, EXPERTS, 2, 2048),
        "priority": jax.vmap(lambda own: jax.random.permutation(own, 2 * ROWS_DEV))(jax.random.split(key_of[7], BLOCKS)).reshape((BLOCKS, 2 * ROWS_DEV)).astype(jnp.int32),
        "w_gate": normal_values(key_of[8], (EXPERTS, D, FF), D ** -0.5, 0.078125, ((0, 8), (2, 32))),
        "w_up": normal_values(key_of[9], (EXPERTS, D, FF), D ** -0.5, 0.078125, ((0, 8), (2, 32))),
        "w_down": normal_values(key_of[10], (EXPERTS, FF, D), FF ** -0.5, 0.0625, ((0, 8), (1, 32))),
    }


eps_norm = 1e-05
masked_score = -1e+30

def row_positions(span_order, row_count, span_size):
    row_index = jnp.arange(row_count, dtype=jnp.int32)
    return span_order[row_index // span_size] * span_size + row_index % span_size

def attend(query_rows, key_rows, value_rows, query_pos, key_pos):
    row_count = query_rows.shape[0]
    key_count = key_rows.shape[0]
    group_size = HEADS // KV_HEADS
    query_heads = query_rows.astype(jnp.float32).reshape(row_count, KV_HEADS, group_size, HD)
    key_heads = key_rows.astype(jnp.float32).reshape(key_count, KV_HEADS, HD)
    value_heads = value_rows.astype(jnp.float32).reshape(key_count, KV_HEADS, HD)
    visible = (key_pos[None, :] <= query_pos[:, None])[None, None]
    scores = jnp.einsum('tjgd,kjd->jgtk', query_heads, key_heads) * HD ** (-0.5)
    scores = jnp.where(visible, scores, masked_score)
    highest = lax.optimization_barrier(jnp.max(scores, axis=3, keepdims=True))
    weights = jnp.where(visible, jnp.exp(scores - highest), 0.0)
    denominator = lax.optimization_barrier(jnp.sum(weights, axis=3))
    rounded = lax.optimization_barrier(weights.astype(jnp.bfloat16))
    weighted = jnp.einsum('jgtk,kjd->jgtd', rounded.astype(jnp.float32), value_heads)
    heads_out = weighted / denominator[..., None]
    return heads_out.transpose(2, 0, 1, 3).reshape(row_count, HEADS * HD).astype(jnp.bfloat16)

def pair_slots(route_rows, order_row, capacity):
    pair_expert = route_rows.reshape(-1)
    same_expert = pair_expert[:, None] == pair_expert[None, :]
    earlier = order_row[None, :] < order_row[:, None]
    pair_rank = lax.optimization_barrier(jnp.sum((same_expert & earlier).astype(jnp.int32), axis=1))
    return (pair_expert * capacity + pair_rank, pair_rank < capacity)

def route_tables(route_rows, order_row, logit_rows, capacity, expert_layers):
    row_count = route_rows.shape[0]
    slot_index, kept_pairs = pair_slots(route_rows, order_row, capacity)
    columns = jnp.arange(expert_layers * capacity, dtype=jnp.int32)
    onehot = ((slot_index[:, None] == columns[None, :]) & kept_pairs[:, None]).astype(jnp.float32)
    onehot = onehot.reshape(row_count, 2, expert_layers * capacity)
    expert_ids = jnp.arange(expert_layers, dtype=jnp.int32)
    picked = lax.optimization_barrier(jnp.sum(jnp.where(route_rows[:, :, None] == expert_ids[None, None, :], logit_rows[:, None, :], 0.0), axis=2))
    shares = jax.nn.sigmoid(picked - picked[:, ::-1])
    return (lax.optimization_barrier(jnp.sum(onehot, axis=1)), lax.optimization_barrier(jnp.sum(onehot * shares[:, :, None], axis=1)))

def expert_apply(operands):
    slot_rows, gate_weight, up_weight, down_weight = operands
    gate_part = jnp.dot(slot_rows, gate_weight, preferred_element_type=jnp.float32)
    up_part = jnp.dot(slot_rows, up_weight, preferred_element_type=jnp.float32)
    hidden = (jax.nn.silu(gate_part) * up_part).astype(jnp.bfloat16)
    block_width = FF // N_CTX
    hidden_blocks = hidden.reshape(slot_rows.shape[0], N_CTX, block_width).transpose(1, 0, 2)
    down_blocks = down_weight.reshape(N_CTX, block_width, D)

    def add_block(running, operand_pair):
        term = jnp.dot(operand_pair[0], operand_pair[1], preferred_element_type=jnp.float32).astype(jnp.bfloat16)
        term = lax.optimization_barrier(term)
        return (running + term.astype(jnp.float32), None)
    summed, unused = lax.scan(add_block, jnp.zeros((slot_rows.shape[0], D), jnp.float32), (hidden_blocks, down_blocks))
    return summed.astype(jnp.bfloat16)

def reference(queries, keys, values, span_order, norm_gain, router_weight, routes, priority, w_gate, w_up, w_down):
    positions = row_positions(span_order, LEN, SPAN)

    def block_rows(array, block_index):
        return lax.dynamic_slice_in_dim(array, (block_index * TOK_DEV).astype(jnp.int32), TOK_DEV, 0)

    def one_block(block_index):
        far_index = ((block_index - 2) % N_CTX).astype(jnp.int32)
        near_index = ((block_index - 1) % N_CTX).astype(jnp.int32)
        order_list = (far_index, near_index, block_index)
        key_rows = jnp.concatenate([block_rows(keys, index_now) for index_now in order_list], axis=0)
        value_rows = jnp.concatenate([block_rows(values, index_now) for index_now in order_list], axis=0)
        key_pos = jnp.concatenate([block_rows(positions, index_now) for index_now in order_list], axis=0)
        return attend(block_rows(queries, block_index), key_rows, value_rows, block_rows(positions, block_index), key_pos)
    attended = lax.map(one_block, jnp.arange(N_CTX, dtype=jnp.int32)).reshape(LEN, D)
    activations = attended.astype(jnp.float32)
    inverse_rms = lax.rsqrt(lax.optimization_barrier(jnp.mean(activations * activations, axis=-1, keepdims=True)) + eps_norm)
    normed = (activations * inverse_rms * norm_gain.astype(jnp.float32)).astype(jnp.bfloat16)
    logits = jnp.einsum('ld,de->le', normed.astype(jnp.float32), router_weight.astype(jnp.float32))
    tables = jax.vmap(partial(route_tables, capacity=CAP, expert_layers=EXPERTS))
    dispatch_mask, combine_weights = tables(routes.reshape(BLOCKS, ROWS_DEV, 2), priority, logits.reshape(BLOCKS, ROWS_DEV, EXPERTS))
    normalized_blocks = normed.reshape(BLOCKS, ROWS_DEV, D).astype(jnp.float32)
    expert_queues = jnp.einsum('suz,sua->sza', dispatch_mask, normalized_blocks).astype(jnp.bfloat16)
    expert_rows = expert_queues.reshape(BLOCKS, EXPERTS, CAP, D).transpose(1, 0, 2, 3).reshape(EXPERTS, BLOCKS * CAP, D)
    outputs = lax.map(expert_apply, (expert_rows, w_gate, w_up, w_down))
    returned_output = outputs.reshape(EXPERTS, BLOCKS, CAP, D).transpose(1, 0, 2, 3).reshape(BLOCKS, EXPERTS * CAP, D)
    expert_blend = jnp.einsum('rni,ris->rns', combine_weights, returned_output.astype(jnp.float32), precision=lax.Precision.HIGHEST)
    layer_out = activations + expert_blend.reshape(LEN, D)
    return layer_out.astype(jnp.bfloat16)
```

```python
import jax
import jax.numpy as jnp
from jax import lax
from jax.experimental import pallas as pl
from jax.experimental.pallas import tpu as pltpu
from jax.sharding import PartitionSpec as P

MESH = pl.DeviceIdType.MESH
BF = jnp.bfloat16
F32 = jnp.float32

HD = 128
HEADS_HERE = 6
TOK = 128
ROWS = 16
SPAN = 64
D = 6144
COLS = 768
EXP = 8
CTX = 32
CAP = 4
PARTS = 4
WIDE = D // PARTS
HID = 256
EPS = 1e-05
MASKED = -1e30


def dot(a, b):
    return jnp.dot(a, b, preferred_element_type=F32)


def kernel(
    q_ref, k_ref, v_ref, span_ref, gain_ref, router_hbm, routes_ref, prio_ref,
    gate_hbm, up_hbm, down_hbm,
    out_ref,
    kv, heads, held, router, normed, sends, arrived, tokens, gate_w, up_w, down_w,
    gate_acc, up_acc, parts, landed, back, returned, logits_ref,
    kv_s, kv_r, hd_s, hd_r, ds_s, ds_r, ag_s, ag_r, rs_s, rs_r, rt_s, rt_r, w_sem,
):
    ctx = lax.axis_index("ctx")
    me = lax.axis_index("exp")
    y = lax.rem(ctx, 4)
    zh = lax.rem(lax.div(ctx, 4), 2)
    x = lax.div(ctx, 8)

    def ctx_at(xx, zz, yy):
        return (xx * 2 + zz) * 4 + yy

    def near(axis, sign):
        step = 1 if sign > 0 else 3
        if axis == "x":
            return (ctx_at(lax.rem(x + step, 4), zh, y), me)
        return (ctx_at(x, zh, lax.rem(y + step, 4)), me)

    other_ctx = ctx_at(x, 1 - zh, y)

    def ring(far, d):
        return (other_ctx if far else ctx, lax.rem(me + d, EXP))

    def after(steps):
        return (lax.rem(ctx + steps + CTX, CTX), me)

    def remote(src, dst, s, r, device):
        return pltpu.make_async_remote_copy(
            src_ref=src, dst_ref=dst, send_sem=s, recv_sem=r,
            device_id=device, device_id_type=MESH,
        )

    weight_copies = [
        pltpu.make_async_copy(router_hbm, router, w_sem.at[0]),
        pltpu.make_async_copy(gate_hbm.at[0], gate_w, w_sem.at[1]),
        pltpu.make_async_copy(up_hbm.at[0], up_w, w_sem.at[2]),
        pltpu.make_async_copy(down_hbm.at[0], down_w, w_sem.at[3]),
    ]

    barrier = pltpu.get_barrier_semaphore()
    greeted = [after(-1), after(-2)]
    greeted += [near(axis, sign) for axis in "xy" for sign in (1, -1)]
    greeted += [ring(far, d) for far in (0, 1) for d in range(EXP) if far or d]
    for device in greeted:
        pl.semaphore_signal(barrier, inc=1, device_id=device, device_id_type=MESH)
    pl.semaphore_wait(barrier, len(greeted))

    kv_copies = []
    for back_steps in (1, 2):
        for which, ref in enumerate((k_ref, v_ref)):
            slot = (back_steps - 1) * 2 + which
            copy = remote(ref, kv.at[slot], kv_s.at[slot], kv_r.at[slot], after(back_steps))
            copy.start()
            kv_copies.append(copy)
    for copy in weight_copies:
        copy.start()

    def span_base(block, half):
        return span_ref[block * 2 + half] * SPAN

    blocks = [lax.rem(ctx + CTX - 2, CTX), lax.rem(ctx + CTX - 1, CTX), ctx]
    lane = lax.broadcasted_iota(jnp.int32, (TOK, 3 * TOK), 1)
    sub = lax.broadcasted_iota(jnp.int32, (TOK, 3 * TOK), 0)
    key_pos = lax.rem(lane, SPAN)
    lane_span = lax.div(lane, SPAN)
    for n in range(6):
        key_pos = key_pos + jnp.where(lane_span == n, span_base(blocks[n // 2], n % 2), 0)
    query_pos = lax.rem(sub, SPAN) + jnp.where(
        sub < SPAN, span_base(ctx, 0), span_base(ctx, 1)
    )
    visible = key_pos <= query_pos

    lane_t = lax.rem(lax.broadcasted_iota(jnp.int32, (ROWS, 64), 1), ROWS)
    pick = lax.broadcasted_iota(jnp.int32, (ROWS, 64), 0) == lane_t
    first = lax.broadcasted_iota(jnp.int32, (ROWS, 64), 1) < ROWS
    lane_32 = lax.broadcasted_iota(jnp.int32, (ROWS, 32), 1)
    sub_32 = lax.broadcasted_iota(jnp.int32, (ROWS, 32), 0)
    routes = routes_ref[...].astype(F32)
    prio = prio_ref[...].astype(F32)
    e_col = [routes[:, k : k + 1] for k in range(2)]
    p_col = [
        jnp.sum(jnp.where(lane_32 == 2 * sub_32 + k, prio, 0.0), axis=1, keepdims=True)
        for k in range(2)
    ]
    e_row = [jnp.sum(jnp.where(pick, e, 0.0), axis=0, keepdims=True) for e in e_col]
    p_row = [jnp.sum(jnp.where(pick, p, 0.0), axis=0, keepdims=True) for p in p_col]
    slot_row, slot_col = [], []
    for k in range(2):
        rank_row = jnp.zeros((1, 64), F32)
        rank_col = jnp.zeros((ROWS, 1), F32)
        for n in range(2):
            rank_row += jnp.sum(
                jnp.where((e_col[n] == e_row[k]) & (p_col[n] < p_row[k]), 1.0, 0.0),
                axis=0, keepdims=True,
            )
            rank_col += jnp.sum(
                jnp.where((e_row[n] == e_col[k]) & (p_row[n] < p_col[k]) & first, 1.0, 0.0),
                axis=1, keepdims=True,
            )
        slot_row.append(jnp.where(rank_row < CAP, e_row[k] * CAP + rank_row, -1.0))
        slot_col.append(jnp.where(rank_col < CAP, e_col[k] * CAP + rank_col, -1.0))

    for copy in kv_copies:
        copy.wait_recv()
    key_blocks = [kv[2], kv[0], k_ref[...]]
    value_blocks = [kv[3], kv[1], v_ref[...]]
    for h in range(HEADS_HERE):
        query = q_ref[:, h * HD : (h + 1) * HD]
        scores = jnp.concatenate(
            [
                lax.dot_general(
                    query, block, (((1,), (1,)), ((), ())), preferred_element_type=F32
                )
                for block in key_blocks
            ],
            axis=1,
        ) * HD ** (-0.5)
        scores = jnp.where(visible, scores, MASKED)
        highest = jnp.max(scores, axis=1, keepdims=True)
        weights = jnp.where(visible, jnp.exp(scores - highest), 0.0)
        denominator = jnp.sum(weights, axis=1, keepdims=True)
        weights = weights.astype(BF)
        total = dot(weights[:, :TOK], value_blocks[0])
        total += dot(weights[:, TOK : 2 * TOK], value_blocks[1])
        total += dot(weights[:, 2 * TOK :], value_blocks[2])
        head = (total / denominator).astype(BF)
        heads[:, :, h * HD : (h + 1) * HD] = head.reshape(EXP, ROWS, HD)

    head_copies = []
    for d in range(1, EXP):
        peer = lax.rem(me + d, EXP)
        copy = remote(heads.at[peer], held.at[me], hd_s.at[d], hd_r.at[d], ring(0, d))
        copy.start()
        head_copies.append(copy)
    held[me] = heads[me]

    lane_64 = lax.broadcasted_iota(jnp.int32, (128, 64), 1)
    row_128 = lax.broadcasted_iota(jnp.int32, (128, 64), 0)
    row_expert = lax.rem(lax.div(row_128, 16) + me, EXP)
    row_slot = (row_expert * CAP + lax.rem(row_128, 4)).astype(F32)
    same_part = lax.rem(lax.div(row_128, 4), 4) == lax.div(lane_64, ROWS)
    dispatch = jnp.where(
        same_part & ((slot_row[0] == row_slot) | (slot_row[1] == row_slot)), 1.0, 0.0
    ).astype(BF)
    row_64 = lax.broadcasted_iota(jnp.int32, (64, 64), 0)
    col_64 = lax.broadcasted_iota(jnp.int32, (64, 64), 1)
    swapped = lax.rem(lax.div(row_64, 4), 4) * 16 + lax.div(row_64, 16) * 4 + lax.rem(row_64, 4)
    swap = jnp.where(col_64 == swapped, 1.0, 0.0).astype(BF)

    for copy in head_copies:
        copy.wait_recv()
    square = jnp.zeros((ROWS, 1), F32)
    for e in range(EXP):
        block = held[e].astype(F32)
        square += jnp.sum(block * block, axis=1, keepdims=True)
    inverse = lax.rsqrt(square * (1.0 / D) + EPS)
    for e in range(EXP):
        block = held[e].astype(F32) * inverse * gain_ref[:, e * COLS : (e + 1) * COLS]
        q0 = e // 2
        normed[q0 * ROWS : (q0 + 1) * ROWS, (e % 2) * COLS : (e % 2 + 1) * COLS] = block.astype(BF)

    sends[...] = dot(dispatch, normed[...]).astype(BF).reshape(EXP, 16, WIDE)
    slot_copies = {}
    for far in (0, 1):
        for d in range(EXP):
            if not far and not d:
                continue
            n = far * EXP + (EXP - d) % EXP
            copy = remote(sends.at[d], arrived.at[n], ds_s.at[n], ds_r.at[n], ring(far, d))
            copy.start()
            slot_copies[n] = copy
    arrived[0] = sends[0]

    weight_copies[0].wait()
    logits = jnp.zeros((ROWS, EXP), F32)
    for e in range(EXP):
        q0 = e // 2
        block = normed[q0 * ROWS : (q0 + 1) * ROWS, (e % 2) * COLS : (e % 2 + 1) * COLS]
        logits += dot(block, router[e * COLS : (e + 1) * COLS, :])
    lane_8 = lax.broadcasted_iota(jnp.int32, (ROWS, EXP), 1).astype(F32)
    picked = [
        jnp.sum(jnp.where(lane_8 == e, logits, 0.0), axis=1, keepdims=True) for e in e_col
    ]
    shares = [
        1.0 / (1.0 + jnp.exp(picked[1] - picked[0])),
        1.0 / (1.0 + jnp.exp(picked[0] - picked[1])),
    ]
    lane_256 = lax.broadcasted_iota(jnp.int32, (64, 256), 1)
    row_b = lax.broadcasted_iota(jnp.int32, (64, 256), 0)
    lane_expert = lax.rem(me + EXP - lax.rem(lax.div(lane_256, 16), EXP), EXP)
    lane_slot = (lane_expert * CAP + lax.rem(lane_256, 4)).astype(F32)
    blend = jnp.zeros((64, 256), F32)
    for k in range(2):
        slot_tall = jnp.concatenate([slot_col[k]] * PARTS, axis=0)
        share_tall = jnp.concatenate([shares[k]] * PARTS, axis=0)
        blend += jnp.where(slot_tall == lane_slot, share_tall, 0.0)
    blend = jnp.where(lax.div(row_b, ROWS) == lax.rem(lax.div(lane_256, 4), 4), blend, 0.0)
    logits_ref[...] = blend

    axes = [("x", "y"), ("y", "x"), ("x", "y"), ("y", "x")]
    first_sign = [1, -1, -1, 1]

    def second_sign(a):
        return 1 if a < 2 else -1

    ag = [dict() for _ in range(4)]

    def at(a, b):
        return a * 4 + b

    def push(k, src, dst, axis, sign):
        copy = remote(
            tokens.at[k, src], tokens.at[k, dst], ag_s.at[k, dst], ag_r.at[k, dst],
            near(axis, sign),
        )
        copy.start()
        ag[k][dst] = copy

    def take_slots(k):
        for m in range(4):
            n = (k // 2) * EXP + (k % 2) * 4 + m
            if n:
                slot_copies[n].wait_recv()
        first_n = (k // 2) * EXP + (k % 2) * 4
        rows = arrived[first_n : first_n + 4].reshape(64, WIDE)
        moved = dot(swap, rows).astype(BF)
        for part in range(PARTS):
            tokens[k, 0, :, part * WIDE : (part + 1) * WIDE] = moved[part * 16 : (part + 1) * 16]

    def spread(k, a):
        push(k, at(a, 0), at(a, 3), axes[k][1], 1)
        push(k, at(a, 0), at(a, 1), axes[k][1], -1)

    def ag_steps(k):
        sign = first_sign[k]

        def own():
            take_slots(k)
            push(k, 0, at(3, 0), axes[k][0], 1)
            push(k, 0, at(1, 0), axes[k][0], -1)
            spread(k, 0)

        def neighbours():
            for a in (3, 1) if sign > 0 else (1, 3):
                ag[k][at(a, 0)].wait_recv()
                if a == (3 if sign > 0 else 1):
                    push(k, at(a, 0), at(2, 0), axes[k][0], sign)
                spread(k, a)

        def onward(a):
            b = 3 if second_sign(a) > 0 else 1

            def go():
                ag[k][at(a, b)].wait_recv()
                push(k, at(a, b), at(a, 2), axes[k][1], second_sign(a))

            return go

        def opposite():
            ag[k][at(2, 0)].wait_recv()
            spread(k, 2)

        def rest():
            for a in range(4):
                ag[k][at(a, 1 if second_sign(a) > 0 else 3)].wait_recv()
            for a in range(4):
                ag[k][at(a, 2)].wait_recv()

        return [own, neighbours, onward(0), opposite, onward(1), onward(3), onward(2), rest]

    def ffn_steps(k):
        def up_step(n):
            def go():
                if k == 0 and n == 0:
                    for copy in weight_copies[1:]:
                        copy.wait()
                columns = slice(n * WIDE, (n + 1) * WIDE)
                rows = tokens[k, :, :, columns].reshape(256, WIDE)
                g = dot(rows, gate_w[columns, :])
                u = dot(rows, up_w[columns, :])
                if n:
                    gate_acc[...] += g
                    up_acc[...] += u
                else:
                    gate_acc[...] = g
                    up_acc[...] = u

            return go

        def down_step(n):
            def go():
                gate = gate_acc[...]
                hidden = (gate / (1.0 + jnp.exp(-gate)) * up_acc[...]).astype(BF)
                columns = slice(n * WIDE, (n + 1) * WIDE)
                parts[k, :, :, columns] = (
                    dot(hidden, down_w[:, columns]).astype(BF).reshape(16, 16, WIDE)
                )

            return go

        return [up_step(n) for n in range(PARTS)] + [down_step(n) for n in range(PARTS)]

    rs = [dict() for _ in range(4)]

    def hand(k, src, n, axis, sign):
        copy = remote(
            parts.at[k, src], landed.at[k, n], rs_s.at[k, n], rs_r.at[k, n], near(axis, sign)
        )
        copy.start()
        rs[k][n] = copy

    def add(k, slot, *ns):
        total = parts[k, slot].astype(F32)
        for n in ns:
            total += landed[k, n].astype(F32)
        parts[k, slot] = total.astype(BF)

    rt = []

    def rs_steps(k):
        sign = first_sign[k]
        mid, opp = (1, 3) if sign > 0 else (3, 1)
        order = [2, mid, opp, 0]

        def begin():
            for a in order:
                s = second_sign(a)
                hand(k, at(a, 2), a * 3, axes[k][1], s)
                hand(k, at(a, 3 if s > 0 else 1), a * 3 + 2, axes[k][1], -s)

        def middle(a):
            def go():
                s = second_sign(a)
                m = at(a, 1 if s > 0 else 3)
                rs[k][a * 3].wait_recv()
                add(k, m, a * 3)
                hand(k, m, a * 3 + 1, axes[k][1], s)

            return go

        def close(a):
            def go():
                rs[k][a * 3 + 1].wait_recv()
                rs[k][a * 3 + 2].wait_recv()
                if a == 2:
                    add(k, at(a, 0), a * 3 + 1, a * 3 + 2)
                    hand(k, at(2, 0), 12, axes[k][0], sign)
                elif a == opp:
                    add(k, at(a, 0), a * 3 + 1, a * 3 + 2)
                    hand(k, at(opp, 0), 14, axes[k][0], -sign)
                elif a == mid:
                    rs[k][12].wait_recv()
                    add(k, at(a, 0), a * 3 + 1, a * 3 + 2, 12)
                    hand(k, at(mid, 0), 13, axes[k][0], sign)
                else:
                    rs[k][13].wait_recv()
                    rs[k][14].wait_recv()
                    add(k, at(a, 0), a * 3 + 1, a * 3 + 2, 13, 14)

            return go

        def give_back():
            rows = jnp.concatenate(
                [parts[k, 0, :, n * WIDE : (n + 1) * WIDE] for n in range(PARTS)], axis=0
            )
            back[k] = dot(swap, rows).astype(BF).reshape(4, 16, WIDE)
            for m in range(4):
                d = (k % 2) * 4 + m
                n = (k // 2) * EXP + d
                if n:
                    copy = remote(
                        back.at[k, m], returned.at[n], rt_s.at[n], rt_r.at[n], ring(k // 2, d)
                    )
                    copy.start()
                    rt.append(copy)
                else:
                    returned[0] = back[k, m]

        return (
            [begin]
            + [middle(a) for a in order]
            + [close(2), close(opp), close(mid), close(0), give_back]
        )

    def run(*lists):
        for n in range(max(len(one) for one in lists)):
            for one in lists:
                if n < len(one):
                    one[n]()

    g = [ag_steps(k) for k in range(4)]
    f = [ffn_steps(k) for k in range(4)]
    r = [rs_steps(k) for k in range(4)]
    run(g[0][:2], g[1][:2])
    run(g[2][:1], g[3][:1])
    run(g[0][2:7], g[1][2:7])
    run(g[2][1:3], g[3][1:3])
    g[0][7]()
    run(f[0], g[2][3:7], g[3][3:7])
    g[1][7]()
    run(f[1])
    run(r[0][:1], r[1][:1])
    g[2][7]()
    run(f[2], r[0][1:5])
    g[3][7]()
    run(f[3], r[1][1:5])
    run(r[2][:1], r[3][:1])
    run(r[0][5:], r[1][5:])
    run(r[2][1:], r[3][1:])

    for copy in rt:
        copy.wait_recv()
    blend = logits_ref[...]
    high = blend.astype(BF)
    low = (blend - high.astype(F32)).astype(BF)
    came = returned[...].reshape(256, WIDE)
    mixed = dot(high, came) + dot(low, came)
    for e in range(EXP):
        q0 = e // 2
        block = mixed[q0 * ROWS : (q0 + 1) * ROWS, (e % 2) * COLS : (e % 2 + 1) * COLS]
        out_ref[:, e * COLS : (e + 1) * COLS] = (held[e].astype(F32) + block).astype(BF)

    for copy in kv_copies + head_copies + list(slot_copies.values()) + rt:
        copy.wait_send()
    for k in range(4):
        for copy in list(ag[k].values()) + list(rs[k].values()):
            copy.wait_send()


def body(
    queries, keys, values, span_order, norm_gain, router_weight, routes, priority,
    w_gate, w_up, w_down,
):
    vmem = pl.BlockSpec(memory_space=pltpu.VMEM)
    smem = pl.BlockSpec(memory_space=pltpu.SMEM)
    hbm = pl.BlockSpec(memory_space=pl.ANY)
    dma = pltpu.SemaphoreType.DMA
    return pl.pallas_call(
        kernel,
        out_shape=jax.ShapeDtypeStruct((ROWS, D), BF),
        in_specs=[vmem, vmem, vmem, smem, vmem, hbm, vmem, vmem, hbm, hbm, hbm],
        out_specs=vmem,
        scratch_shapes=[
            pltpu.VMEM((4, TOK, HD), BF),
            pltpu.VMEM((EXP, ROWS, COLS), BF),
            pltpu.VMEM((EXP, ROWS, COLS), BF),
            pltpu.VMEM((D, EXP), BF),
            pltpu.VMEM((64, WIDE), BF),
            pltpu.VMEM((EXP, 16, WIDE), BF),
            pltpu.VMEM((2 * EXP, 16, WIDE), BF),
            pltpu.VMEM((4, 16, 16, D), BF),
            pltpu.VMEM((D, HID), BF),
            pltpu.VMEM((D, HID), BF),
            pltpu.VMEM((HID, D), BF),
            pltpu.VMEM((256, HID), F32),
            pltpu.VMEM((256, HID), F32),
            pltpu.VMEM((4, 16, 16, D), BF),
            pltpu.VMEM((4, 15, 16, D), BF),
            pltpu.VMEM((4, 4, 16, WIDE), BF),
            pltpu.VMEM((2 * EXP, 16, WIDE), BF),
            pltpu.VMEM((64, 256), F32),
            dma((4,)), dma((4,)),
            dma((EXP,)), dma((EXP,)),
            dma((2 * EXP,)), dma((2 * EXP,)),
            dma((4, 16)), dma((4, 16)),
            dma((4, 15)), dma((4, 15)),
            dma((2 * EXP,)), dma((2 * EXP,)),
            dma((4,)),
        ],
        compiler_params=pltpu.CompilerParams(
            collective_id=0, has_side_effects=True, vmem_limit_bytes=60 * 1024 * 1024
        ),
    )(
        queries, keys, values, span_order, norm_gain.astype(F32).reshape(1, D),
        router_weight, routes, priority, w_gate, w_up, w_down,
    )


def solution(mesh):
    placed = (
        P("ctx", "exp"),
        P("ctx", "exp"),
        P("ctx", "exp"),
        P(),
        P(),
        P(),
        P(("ctx", "exp"), None),
        P(("ctx", "exp"), None),
        P("exp", None, "ctx"),
        P("exp", None, "ctx"),
        P("exp", "ctx", None),
    )
    return jax.shard_map(
        body, mesh=mesh, in_specs=placed, out_specs=P(("ctx", "exp"), None), check_vma=False
    )
```

```python
import jax
import jax.numpy as jnp
from jax import lax
from jax.experimental import pallas as pl
from jax.experimental.pallas import tpu as pltpu
from jax.sharding import PartitionSpec as P

MESH = pl.DeviceIdType.MESH
BF = jnp.bfloat16
F32 = jnp.float32

HD = 128
HEADS_HERE = 6
TOK = 128
ROWS = 16
SPAN = 64
D = 6144
COLS = 768
EXP = 8
CTX = 32
CAP = 4
PARTS = 4
WIDE = D // PARTS
HALVES = 2
HALF = D // HALVES
NARROW = HALF // PARTS
GROUPS = 2
GROUP_HEADS = HEADS_HERE // GROUPS
GROUP_COLS = GROUP_HEADS * HD
HID = 256
CROSSING = (0, 3)
OVER = (2, 1)
ORDER = (
    (0, 0), (1, 0, 0), (2, 0), (1, 0, 3), (0, 1), (1, 1, 0), (1, 0, 1), (1, 0, 2), (3, 1, 0),
    (2, 1), (1, 1, 3), (1, 1, 1), (3, 0, 0), (0, 2), (0, 3), (1, 2, 0), (1, 3, 0), (4, 3, 0),
    (3, 1, 3), (4, 2, 0), (1, 1, 2), (3, 0, 3), (3, 0, 1), (2, 2), (1, 2, 1), (2, 3), (1, 3, 1),
    (1, 3, 3), (1, 2, 3), (4, 3, 3), (4, 2, 3), (3, 0, 2), (3, 1, 1), (3, 2, 1), (1, 2, 2),
    (3, 3, 1), (3, 1, 2), (1, 3, 2), (5, 0, 0), (5, 0, 1), (5, 0, 2), (5, 0, 3), (5, 0, 4),
    (5, 0, 5), (5, 0, 6), (5, 0, 7), (9, 0, 1, 2), (9, 0, 0, 2), (9, 0, 1, 1), (9, 0, 0, 1),
    (7, 0, 1, 3), (7, 0, 0, 3), (7, 0, 1, 0), (7, 0, 0, 0), (6, 0, 1, 2), (6, 0, 0, 2),
    (6, 0, 1, 1), (6, 0, 0, 1), (3, 2, 2), (5, 1, 0), (5, 1, 1), (5, 1, 2), (5, 1, 3), (5, 1, 4),
    (5, 1, 5), (9, 1, 0, 2), (5, 1, 6), (5, 1, 7), (9, 1, 1, 2), (9, 1, 1, 1), (9, 1, 0, 1),
    (7, 1, 1, 3), (7, 1, 0, 3), (8, 0, 1, 2), (8, 1, 1, 2), (8, 1, 0, 2), (7, 1, 1, 0),
    (7, 1, 0, 0), (8, 0, 1, 1), (6, 1, 1, 2), (6, 1, 0, 2), (6, 1, 1, 1), (6, 1, 0, 1), (3, 3, 2),
    (8, 0, 0, 2), (9, 0, 1, 3), (8, 0, 1, 3), (9, 0, 0, 3), (9, 0, 1, 0), (8, 1, 1, 1),
    (8, 1, 1, 3), (8, 0, 0, 1), (9, 1, 1, 3), (9, 0, 0, 0), (10, 1, 1, 2), (5, 2, 0), (5, 2, 1),
    (9, 1, 0, 3), (5, 2, 2), (5, 2, 3), (5, 2, 4), (5, 2, 5), (5, 2, 6), (5, 2, 7), (7, 2, 1, 2),
    (9, 1, 1, 0), (7, 2, 0, 2), (7, 2, 1, 3), (8, 1, 0, 3), (8, 0, 0, 3), (8, 1, 0, 1),
    (7, 2, 0, 3), (8, 2, 1, 2), (10, 0, 1, 2), (10, 0, 0, 2), (5, 3, 0), (5, 3, 1), (9, 1, 0, 0),
    (5, 3, 2), (5, 3, 3), (5, 3, 4), (5, 3, 5), (5, 3, 6), (5, 3, 7), (7, 2, 1, 1), (7, 3, 1, 3),
    (7, 3, 0, 3), (8, 2, 0, 2), (10, 1, 0, 2), (7, 2, 1, 0), (7, 3, 1, 0), (7, 2, 0, 0),
    (7, 3, 0, 0), (8, 1, 1, 0), (10, 0, 1, 3), (10, 1, 1, 1), (10, 1, 1, 3), (10, 0, 0, 3),
    (9, 2, 1, 2), (10, 1, 0, 1), (7, 2, 0, 1), (10, 0, 1, 1), (9, 2, 0, 2), (9, 3, 1, 3),
    (9, 2, 1, 1), (10, 0, 0, 1), (9, 2, 1, 3), (9, 3, 0, 3), (7, 3, 1, 2), (9, 2, 0, 3),
    (8, 3, 1, 2), (9, 2, 1, 0), (9, 3, 1, 0), (10, 1, 0, 3), (9, 2, 0, 0), (8, 1, 0, 0),
    (9, 3, 0, 0), (7, 3, 0, 2), (10, 1, 1, 0), (11, 1, 1), (10, 2, 1, 2), (8, 3, 0, 2),
    (8, 0, 1, 0), (8, 2, 1, 3), (10, 2, 0, 2), (8, 3, 1, 3), (8, 0, 0, 0), (9, 2, 0, 1),
    (7, 3, 1, 1), (8, 2, 1, 1), (9, 3, 1, 2), (8, 2, 0, 3), (8, 3, 0, 3), (8, 2, 0, 1),
    (8, 3, 1, 1), (10, 1, 0, 0), (11, 1, 0), (9, 3, 0, 2), (7, 3, 0, 1), (8, 2, 1, 0),
    (10, 0, 1, 0), (11, 0, 1), (8, 2, 0, 0), (10, 2, 1, 3), (10, 3, 1, 3), (10, 0, 0, 0),
    (11, 0, 0), (8, 3, 0, 1), (9, 3, 1, 1), (10, 2, 1, 1), (10, 3, 1, 2), (10, 2, 0, 3),
    (10, 3, 0, 3), (10, 2, 0, 1), (8, 3, 1, 0), (9, 3, 0, 1), (10, 3, 0, 2), (8, 3, 0, 0),
    (10, 3, 1, 1), (10, 2, 1, 0), (11, 2, 1), (10, 2, 0, 0), (11, 2, 0), (10, 3, 0, 1),
    (10, 3, 1, 0), (11, 3, 1), (10, 3, 0, 0), (11, 3, 0),
)
EPS = 1e-05
MASKED = -1e30


def dot(a, b):
    return jnp.dot(a, b, preferred_element_type=F32)


def kernel(
    q_ref, k_ref, v_ref, span_ref, gain_ref, router_ref, routes_ref, prio_ref,
    gate_hbm, up_hbm, down_hbm,
    out_ref,
    kv, own_scores, heads, held, normed, sends, arrived, tokens, gate_w, up_w, down_w,
    gate_acc, up_acc, hidden, parts, landed, crossed, back, returned, blend_ref,
    kv_s, kv_r, hd_s, hd_r, ds_s, ds_r, ag_s, ag_r, rs_s, rs_r, ov_s, ov_r, rt_s, rt_r, w_sem,
):
    ctx = lax.axis_index("ctx")
    me = lax.axis_index("exp")
    y = lax.rem(ctx, 4)
    zh = lax.rem(lax.div(ctx, 4), 2)
    x = lax.div(ctx, 8)

    def ctx_at(xx, zz, yy):
        return (xx * 2 + zz) * 4 + yy

    def near(axis, sign):
        step = 1 if sign > 0 else 3
        if axis == "x":
            return (ctx_at(lax.rem(x + step, 4), zh, y), me)
        return (ctx_at(x, zh, lax.rem(y + step, 4)), me)

    other_ctx = ctx_at(x, 1 - zh, y)

    bits = [lax.rem(me, 2), lax.rem(lax.div(me, 2), 2), lax.div(me, 4)]

    def partner(d):
        flipped = [1 - bit if d >> n & 1 else bit for n, bit in enumerate(bits)]
        return flipped[0] + 2 * flipped[1] + 4 * flipped[2]

    def ring(far, d):
        return (other_ctx if far else ctx, partner(d))

    def after(steps):
        return (lax.rem(ctx + steps + CTX, CTX), me)

    def remote(src, dst, s, r, device):
        return pltpu.make_async_remote_copy(
            src_ref=src, dst_ref=dst, send_sem=s, recv_sem=r,
            device_id=device, device_id_type=MESH,
        )

    weight_copies = [
        pltpu.make_async_copy(gate_hbm.at[0], gate_w, w_sem.at[0]),
        pltpu.make_async_copy(up_hbm.at[0], up_w, w_sem.at[1]),
        pltpu.make_async_copy(down_hbm.at[0], down_w, w_sem.at[2]),
    ]

    barrier = pltpu.get_barrier_semaphore()
    greeted = [after(-1), after(-2)]
    greeted += [ring(0, d) for d in range(1, EXP)]
    greeted += [near(axis, sign) for axis in "xy" for sign in (1, -1)]
    greeted += [ring(1, d) for d in range(EXP)]
    for device in greeted:
        pl.semaphore_signal(barrier, inc=1, device_id=device, device_id_type=MESH)

    def span_base(block, half):
        return span_ref[block * 2 + half] * SPAN

    blocks = [lax.rem(ctx + CTX - 2, CTX), lax.rem(ctx + CTX - 1, CTX), ctx]
    lane = lax.broadcasted_iota(jnp.int32, (TOK, 3 * TOK), 1)
    sub = lax.broadcasted_iota(jnp.int32, (TOK, 3 * TOK), 0)
    key_pos = lax.rem(lane, SPAN)
    lane_span = lax.div(lane, SPAN)
    for n in range(6):
        key_pos = key_pos + jnp.where(lane_span == n, span_base(blocks[n // 2], n % 2), 0)
    query_pos = lax.rem(sub, SPAN) + jnp.where(
        sub < SPAN, span_base(ctx, 0), span_base(ctx, 1)
    )
    visible = key_pos <= query_pos

    lane_t = lax.rem(lax.broadcasted_iota(jnp.int32, (ROWS, 64), 1), ROWS)
    pick = lax.broadcasted_iota(jnp.int32, (ROWS, 64), 0) == lane_t
    first = lax.broadcasted_iota(jnp.int32, (ROWS, 64), 1) < ROWS
    lane_16 = lax.broadcasted_iota(jnp.int32, (ROWS, ROWS), 1)
    sub_16 = lax.broadcasted_iota(jnp.int32, (ROWS, ROWS), 0)
    lane_32 = lax.broadcasted_iota(jnp.int32, (ROWS, 32), 1)
    sub_32 = lax.broadcasted_iota(jnp.int32, (ROWS, 32), 0)
    routes = routes_ref[...].astype(F32)
    prio = prio_ref[...].astype(F32)
    e_col = [
        jnp.sum(jnp.where(lane_16 == sub_16, routes[k : k + 1, :], 0.0), axis=1, keepdims=True)
        for k in range(2)
    ]
    p_col = [
        jnp.sum(jnp.where(lane_32 == 2 * sub_32 + k, prio, 0.0), axis=1, keepdims=True)
        for k in range(2)
    ]
    e_row = [jnp.sum(jnp.where(pick, e, 0.0), axis=0, keepdims=True) for e in e_col]
    p_row = [jnp.sum(jnp.where(pick, p, 0.0), axis=0, keepdims=True) for p in p_col]
    slot_row, slot_col = [], []
    for k in range(2):
        rank_row = jnp.zeros((1, 64), F32)
        rank_col = jnp.zeros((ROWS, 1), F32)
        for n in range(2):
            rank_row += jnp.sum(
                jnp.where((e_col[n] == e_row[k]) & (p_col[n] < p_row[k]), 1.0, 0.0),
                axis=0, keepdims=True,
            )
            rank_col += jnp.sum(
                jnp.where((e_row[n] == e_col[k]) & (p_row[n] < p_col[k]) & first, 1.0, 0.0),
                axis=1, keepdims=True,
            )
        slot_row.append(jnp.where(rank_row < CAP, e_row[k] * CAP + rank_row, -1.0))
        slot_col.append(jnp.where(rank_col < CAP, e_col[k] * CAP + rank_col, -1.0))

    lane_64 = lax.broadcasted_iota(jnp.int32, (128, 64), 1)
    row_128 = lax.broadcasted_iota(jnp.int32, (128, 64), 0)
    row_expert = lax.bitwise_xor(lax.div(row_128, 16), jnp.full_like(row_128, me))
    row_slot = (row_expert * CAP + lax.rem(row_128, 4)).astype(F32)
    same_part = lax.rem(lax.div(row_128, 4), 4) == lax.div(lane_64, ROWS)
    dispatch = jnp.where(
        same_part & ((slot_row[0] == row_slot) | (slot_row[1] == row_slot)), 1.0, 0.0
    ).astype(BF)
    row_64 = lax.broadcasted_iota(jnp.int32, (64, 64), 0)
    col_64 = lax.broadcasted_iota(jnp.int32, (64, 64), 1)
    swapped = lax.rem(lax.div(row_64, 4), 4) * 16 + lax.div(row_64, 16) * 4 + lax.rem(row_64, 4)
    swap = jnp.where(col_64 == swapped, 1.0, 0.0).astype(BF)

    def score(h, block):
        return lax.dot_general(
            q_ref[:, h * HD : (h + 1) * HD], block, (((1,), (1,)), ((), ())),
            preferred_element_type=F32,
        )

    for h in range(HEADS_HERE):
        own_scores[h] = score(h, k_ref[...])
    pl.semaphore_wait(barrier, len(greeted))

    kv_copies = []
    for which, ref in enumerate((k_ref, v_ref)):
        for back_steps in (1, 2):
            slot = which * 2 + back_steps - 1
            copy = remote(ref, kv.at[slot], kv_s.at[slot], kv_r.at[slot], after(back_steps))
            copy.start()
            kv_copies.append(copy)
    for copy in weight_copies:
        copy.start()

    head_copies = []
    for group in range(GROUPS):
        weights, denominators = [], []
        for h in range(group * GROUP_HEADS, (group + 1) * GROUP_HEADS):
            if h == 0:
                kv_copies[0].wait_recv()
                kv_copies[1].wait_recv()
            scores = jnp.concatenate(
                [score(h, kv[1]), score(h, kv[0]), own_scores[h]], axis=1
            ) * HD ** (-0.5)
            scores = jnp.where(visible, scores, MASKED)
            highest = jnp.max(scores, axis=1, keepdims=True)
            weight = jnp.where(visible, jnp.exp(scores - highest), 0.0)
            denominators.append(jnp.sum(weight, axis=1, keepdims=True))
            weights.append(weight.astype(BF))
        if group == 0:
            kv_copies[2].wait_recv()
            kv_copies[3].wait_recv()
        for n in range(GROUP_HEADS):
            total = dot(weights[n][:, :TOK], kv[3])
            total += dot(weights[n][:, TOK : 2 * TOK], kv[2])
            total += dot(weights[n][:, 2 * TOK :], v_ref[...])
            head = (total / denominators[n]).astype(BF)
            heads[group, :, :, n * HD : (n + 1) * HD] = head.reshape(EXP, ROWS, HD)
        for d in range(1, EXP):
            copy = remote(
                heads.at[group, partner(d)], held.at[group, me],
                hd_s.at[group, d], hd_r.at[group, d], ring(0, d),
            )
            copy.start()
            head_copies.append(copy)
        held[group, me] = heads[group, me]

    for copy in head_copies:
        copy.wait_recv()
    square = jnp.zeros((ROWS, 1), F32)
    for e in range(EXP):
        for group in range(GROUPS):
            block = held[group, e].astype(F32)
            square += jnp.sum(block * block, axis=1, keepdims=True)
    inverse = lax.rsqrt(square * (1.0 / D) + EPS)
    gain = gain_ref[...].astype(F32)
    for n in range(D // HD):
        e, h = n // HEADS_HERE, n % HEADS_HERE
        first_lane = h % GROUP_HEADS * HD
        block = held[h // GROUP_HEADS, e, :, first_lane : first_lane + HD].astype(F32)
        block = block * inverse * gain[n : n + 1, :]
        part, column = n // 12, n % 12 * HD
        normed[part * ROWS : (part + 1) * ROWS, column : column + HD] = block.astype(BF)

    sends[...] = dot(dispatch, normed[...]).astype(BF).reshape(EXP, 16, WIDE)
    slot_copies = {}

    def send_slots(far):
        for d in range(EXP):
            if not far and not d:
                continue
            n = far * EXP + d
            copy = remote(sends.at[d], arrived.at[n], ds_s.at[n], ds_r.at[n], ring(far, d))
            copy.start()
            slot_copies[n] = copy

    send_slots(0)
    arrived[0] = sends[0]

    def make_blend():
        logits = jnp.zeros((ROWS, EXP), F32)
        for part in range(PARTS):
            logits += lax.dot_general(
                normed[part * ROWS : (part + 1) * ROWS, :],
                router_ref[:, part * WIDE : (part + 1) * WIDE],
                (((1,), (1,)), ((), ())), preferred_element_type=F32,
            )
        lane_8 = lax.broadcasted_iota(jnp.int32, (ROWS, EXP), 1).astype(F32)
        picked = [
            jnp.sum(jnp.where(lane_8 == e, logits, 0.0), axis=1, keepdims=True) for e in e_col
        ]
        shares = [
            1.0 / (1.0 + jnp.exp(picked[1] - picked[0])),
            1.0 / (1.0 + jnp.exp(picked[0] - picked[1])),
        ]
        lane_256 = lax.broadcasted_iota(jnp.int32, (64, 256), 1)
        row_b = lax.broadcasted_iota(jnp.int32, (64, 256), 0)
        lane_expert = lax.bitwise_xor(
            lax.rem(lax.div(lane_256, 16), EXP), jnp.full_like(lane_256, me)
        )
        lane_slot = (lane_expert * CAP + lax.rem(lane_256, 4)).astype(F32)
        blend = jnp.zeros((64, 256), F32)
        for k in range(2):
            slot_tall = jnp.concatenate([slot_col[k]] * PARTS, axis=0)
            share_tall = jnp.concatenate([shares[k]] * PARTS, axis=0)
            blend += jnp.where(slot_tall == lane_slot, share_tall, 0.0)
        blend_ref[...] = jnp.where(
            lax.div(row_b, ROWS) == lax.rem(lax.div(lane_256, 4), 4), blend, 0.0
        )

    axes = [("x", "y"), ("y", "x"), ("x", "y"), ("y", "x")]
    first_sign = [1, -1, -1, 1]

    def second_sign(a):
        return 1 if a < 2 else -1

    def at(a, b):
        return a * 4 + b

    copies = {}

    def gather_copy(k, slot):
        a, b = divmod(slot, 4)
        if b:
            axis = axes[k][1]
            if b == 2:
                sign = second_sign(a)
                src = at(a, 3 if sign > 0 else 1)
            else:
                sign = 1 if b == 3 else -1
                src = at(a, 0)
        else:
            axis = axes[k][0]
            if a == 2:
                sign = first_sign[k]
                src = at(3 if sign > 0 else 1, 0)
            else:
                sign = 1 if a == 3 else -1
                src = 0
        if k >= 2 and b == 2 and a in CROSSING:
            src_ref, device = tokens.at[k - 2, slot], (other_ctx, me)
        else:
            src_ref, device = tokens.at[k, src], near(axis, sign)
        return remote(src_ref, tokens.at[k, slot], ag_s.at[k, slot], ag_r.at[k, slot], device)

    def sum_copy(k, c, n):
        if n < 12:
            a, kind = divmod(n, 3)
            axis, sign = axes[k][1], second_sign(a)
            ahead, behind = (1, 3) if sign > 0 else (3, 1)
            src = at(a, (2, ahead, behind)[kind])
        else:
            kind, axis, sign = n - 12, axes[k][0], first_sign[k]
            ahead, behind = (1, 3) if sign > 0 else (3, 1)
            src = at((2, ahead, behind)[kind], 0)
        return remote(
            parts.at[k, c, src], landed.at[k, c, n], rs_s.at[k, c, n], rs_r.at[k, c, n],
            near(axis, -sign if kind == 2 else sign),
        )

    def over_copy(k, c, a):
        n = OVER.index(a)
        return remote(
            parts.at[k, c, at(a, 2)], crossed.at[k, c, n], ov_s.at[k, c, n], ov_r.at[k, c, n],
            (other_ctx, me),
        )

    makers = {"gather": gather_copy, "sum": sum_copy, "over": over_copy}
    waited = set()

    def copy_of(*key):
        if key not in copies:
            copies[key] = makers[key[0]](*key[1:])
        return copies[key]

    def arrival(*key):
        if key not in waited:
            waited.add(key)
            copy_of(*key).wait_recv()

    def take_slots(k):
        first_n = (k // 2) * EXP + (k % 2) * 4
        for n in range(first_n, first_n + 4):
            if n:
                slot_copies[n].wait_recv()
        rows = arrived[first_n : first_n + 4].reshape(64, WIDE)
        moved = dot(swap, rows).astype(BF)
        for part in range(PARTS):
            tokens[k, 0, :, part * WIDE : (part + 1) * WIDE] = moved[part * 16 : (part + 1) * 16]

    def own(k):
        take_slots(k)
        copy_of("gather", k, at(3, 0)).start()
        copy_of("gather", k, at(1, 0)).start()
        if k == 1:
            send_slots(1)
            make_blend()

    def spread(k, a):
        if a:
            arrival("gather", k, at(a, 0))
        copy_of("gather", k, at(a, 3)).start()
        copy_of("gather", k, at(a, 1)).start()

    def forward(k):
        arrival("gather", k, at(3 if first_sign[k] > 0 else 1, 0))
        copy_of("gather", k, at(2, 0)).start()

    def onward(k, a):
        arrival("gather", k, at(a, 3 if second_sign(a) > 0 else 1))
        copy_of("gather", k, at(a, 2)).start()

    def cross(k, a):
        arrival("gather", k - 2, at(a, 2))
        copy_of("gather", k, at(a, 2)).start()

    def ffn(k, n):
        if n == 0:
            for slot in range(1, 16):
                arrival("gather", k, slot)
            if k == 0:
                for copy in weight_copies:
                    copy.wait()
        if n < PARTS:
            columns = slice(n * WIDE, (n + 1) * WIDE)
            rows = tokens[k, :, :, columns].reshape(256, WIDE)
            gate = dot(rows, gate_w[columns, :])
            up = dot(rows, up_w[columns, :])
            if n:
                gate = gate_acc[...] + gate
                up = up_acc[...] + up
            if n == PARTS - 1:
                hidden[...] = (gate / (1.0 + jnp.exp(-gate)) * up).astype(BF)
            else:
                gate_acc[...] = gate
                up_acc[...] = up
        else:
            column = (n - PARTS) * WIDE
            first_column = column % HALF
            parts[k, column // HALF, :, :, first_column : first_column + WIDE] = (
                dot(hidden[...], down_w[:, column : column + WIDE])
                .astype(BF).reshape(16, 16, WIDE)
            )

    def add(k, c, slot, *ns):
        total = parts[k, c, slot].astype(F32)
        for n in ns:
            arrival("sum", k, c, n)
            total += landed[k, c, n].astype(F32)
        parts[k, c, slot] = total.astype(BF)

    def over(k, c, a):
        copy_of("over", k, c, a).start()

    def far(k, c, a):
        if k >= 2 and a in OVER:
            arrival("over", k - 2, c, a)
            total = parts[k, c, at(a, 2)].astype(F32)
            total += crossed[k - 2, c, OVER.index(a)].astype(F32)
            parts[k, c, at(a, 2)] = total.astype(BF)
        copy_of("sum", k, c, a * 3).start()

    def side(k, c, a):
        copy_of("sum", k, c, a * 3 + 2).start()

    def middle(k, c, a):
        if k >= 2 or a not in OVER:
            add(k, c, at(a, 1 if second_sign(a) > 0 else 3), a * 3)
        copy_of("sum", k, c, a * 3 + 1).start()

    def close(k, c, a):
        ahead = 1 if first_sign[k] > 0 else 3
        more = {2: (), ahead: (12,), 4 - ahead: (), 0: (13, 14)}[a]
        add(k, c, at(a, 0), a * 3 + 1, a * 3 + 2, *more)
        if a:
            copy_of("sum", k, c, {2: 12, ahead: 13, 4 - ahead: 14}[a]).start()

    rt = {}

    def give(k, c):
        rows = jnp.concatenate(
            [parts[k, c, 0, :, n * NARROW : (n + 1) * NARROW] for n in range(PARTS)], axis=0
        )
        back[k, c] = dot(swap, rows).astype(BF).reshape(4, 16, NARROW)
        for m in range(4):
            d = (k % 2) * 4 + m
            n = (k // 2) * EXP + d
            if n:
                copy = remote(
                    back.at[k, c, m], returned.at[c, n], rt_s.at[c, n], rt_r.at[c, n],
                    ring(k // 2, d),
                )
                copy.start()
                rt[c, n] = copy
            else:
                returned[c, 0] = back[k, c, m]

    steps = [own, spread, forward, onward, cross, ffn, over, far, side, middle, close, give]
    for which, *where in ORDER:
        steps[which](*where)

    high = blend_ref[...].astype(BF)
    low = (blend_ref[...] - high.astype(F32)).astype(BF)
    for c in range(HALVES):
        for n in range(1, 2 * EXP):
            rt[c, n].wait_recv()
        came = returned[c].reshape(256, NARROW)
        mixed = dot(high, came) + dot(low, came)
        for part in range(PARTS):
            e = c * PARTS + part
            for group in range(GROUPS):
                columns = slice(group * GROUP_COLS, (group + 1) * GROUP_COLS)
                block = mixed[part * ROWS : (part + 1) * ROWS, columns]
                first_column = e * COLS + group * GROUP_COLS
                out_ref[:, first_column : first_column + GROUP_COLS] = (
                    held[group, e].astype(F32) + block
                ).astype(BF)

    for copy in kv_copies + head_copies + list(slot_copies.values()) + list(rt.values()):
        copy.wait_send()
    for copy in copies.values():
        copy.wait_send()


def body(
    queries, keys, values, span_order, norm_gain, router_weight, routes, priority,
    w_gate, w_up, w_down,
):
    vmem = pl.BlockSpec(memory_space=pltpu.VMEM)
    smem = pl.BlockSpec(memory_space=pltpu.SMEM)
    hbm = pl.BlockSpec(memory_space=pl.ANY)
    dma = pltpu.SemaphoreType.DMA
    return pl.pallas_call(
        kernel,
        out_shape=jax.ShapeDtypeStruct((ROWS, D), BF),
        in_specs=[vmem, vmem, vmem, smem, vmem, vmem, vmem, vmem, hbm, hbm, hbm],
        out_specs=vmem,
        scratch_shapes=[
            pltpu.VMEM((4, TOK, HD), BF),
            pltpu.VMEM((HEADS_HERE, TOK, TOK), F32),
            pltpu.VMEM((GROUPS, EXP, ROWS, GROUP_COLS), BF),
            pltpu.VMEM((GROUPS, EXP, ROWS, GROUP_COLS), BF),
            pltpu.VMEM((64, WIDE), BF),
            pltpu.VMEM((EXP, 16, WIDE), BF),
            pltpu.VMEM((2 * EXP, 16, WIDE), BF),
            pltpu.VMEM((4, 16, 16, D), BF),
            pltpu.VMEM((D, HID), BF),
            pltpu.VMEM((D, HID), BF),
            pltpu.VMEM((HID, D), BF),
            pltpu.VMEM((256, HID), F32),
            pltpu.VMEM((256, HID), F32),
            pltpu.VMEM((256, HID), BF),
            pltpu.VMEM((4, HALVES, 16, 16, HALF), BF),
            pltpu.VMEM((4, HALVES, 15, 16, HALF), BF),
            pltpu.VMEM((2, HALVES, len(OVER), 16, HALF), BF),
            pltpu.VMEM((4, HALVES, 4, 16, NARROW), BF),
            pltpu.VMEM((HALVES, 2 * EXP, 16, NARROW), BF),
            pltpu.VMEM((64, 256), F32),
            dma((4,)), dma((4,)),
            dma((GROUPS, EXP)), dma((GROUPS, EXP)),
            dma((2 * EXP,)), dma((2 * EXP,)),
            dma((4, 16)), dma((4, 16)),
            dma((4, HALVES, 15)), dma((4, HALVES, 15)),
            dma((2, HALVES, len(OVER))), dma((2, HALVES, len(OVER))),
            dma((HALVES, 2 * EXP)), dma((HALVES, 2 * EXP)),
            dma((3,)),
        ],
        compiler_params=pltpu.CompilerParams(
            collective_id=0, has_side_effects=True, vmem_limit_bytes=60 * 1024 * 1024
        ),
    )(
        queries, keys, values, span_order, norm_gain.reshape(D // HD, HD),
        router_weight.T, routes.T, priority, w_gate, w_up, w_down,
    )


def solution(mesh):
    placed = (
        P("ctx", "exp"),
        P("ctx", "exp"),
        P("ctx", "exp"),
        P(),
        P(),
        P(),
        P(("ctx", "exp"), None),
        P(("ctx", "exp"), None),
        P("exp", None, "ctx"),
        P("exp", None, "ctx"),
        P("exp", "ctx", None),
    )
    return jax.shard_map(
        body, mesh=mesh, in_specs=placed, out_specs=P(("ctx", "exp"), None), check_vma=False
    )
```

```python
import jax
import jax.numpy as jnp
from jax import lax
from jax.experimental import pallas as pl
from jax.experimental.pallas import tpu as pltpu
from jax.sharding import PartitionSpec as P

MESH = pl.DeviceIdType.MESH
BF = jnp.bfloat16
F32 = jnp.float32

HD = 128
HEADS_HERE = 6
TOK = 128
ROWS = 16
SPAN = 64
D = 6144
COLS = 768
EXP = 8
CTX = 32
CAP = 4
PARTS = 4
WIDE = D // PARTS
HALVES = 2
HALF = D // HALVES
NARROW = HALF // PARTS
GROUPS = 2
GROUP_HEADS = HEADS_HERE // GROUPS
GROUP_COLS = GROUP_HEADS * HD
HID = 256
CROSSING = (0, 3)
OVER = (2, 1)
ORDER = (
    (0, 0), (1, 0, 0), (0, 1), (3, 0, 0), (1, 1, 0), (2, 0), (1, 0, 1), (1, 1, 1), (2, 1),
    (3, 1, 0), (1, 1, 3), (0, 2), (1, 0, 3), (0, 3), (4, 2, 0), (3, 0, 1), (1, 0, 2), (1, 1, 2),
    (3, 0, 3), (4, 3, 0), (2, 2), (3, 1, 1), (3, 0, 2), (3, 1, 3), (1, 3, 3), (2, 3), (1, 2, 2),
    (3, 1, 2), (1, 2, 1), (1, 3, 1), (4, 2, 3), (5, 0, 0), (5, 0, 1), (4, 3, 3), (1, 3, 2),
    (5, 0, 2), (5, 0, 3), (5, 0, 4), (1, 2, 3), (5, 0, 5), (5, 0, 6), (9, 0, 0, 2), (3, 2, 1),
    (1, 2, 0), (5, 0, 7), (5, 1, 0), (6, 0, 0, 1), (5, 1, 1), (3, 3, 1), (5, 1, 2), (5, 1, 3),
    (5, 1, 4), (5, 1, 5), (1, 3, 0), (8, 0, 1, 3), (7, 1, 0, 3), (8, 1, 0, 0), (8, 0, 0, 2),
    (3, 2, 2), (5, 1, 6), (7, 0, 1, 3), (5, 1, 7), (7, 1, 0, 0), (3, 3, 2), (7, 0, 0, 0),
    (9, 1, 0, 2), (8, 1, 1, 2), (7, 0, 0, 3), (8, 0, 0, 1), (8, 0, 1, 0), (8, 1, 0, 1),
    (6, 1, 0, 2), (9, 1, 0, 1), (8, 1, 0, 2), (8, 0, 1, 1), (9, 1, 0, 0), (7, 1, 1, 0), (5, 2, 0),
    (5, 2, 1), (9, 1, 0, 3), (9, 0, 0, 1), (8, 1, 0, 3), (8, 0, 1, 2), (5, 2, 2), (8, 0, 0, 3),
    (5, 2, 3), (6, 1, 0, 1), (5, 2, 4), (9, 0, 0, 0), (7, 0, 1, 0), (5, 2, 5), (9, 0, 1, 1),
    (7, 1, 1, 3), (5, 2, 6), (5, 2, 7), (5, 3, 0), (6, 1, 1, 2), (8, 2, 1, 2), (5, 3, 1),
    (9, 0, 1, 3), (10, 0, 0, 2), (5, 3, 2), (5, 3, 3), (5, 3, 4), (5, 3, 5), (6, 0, 0, 2),
    (8, 2, 0, 1), (6, 0, 1, 2), (7, 3, 0, 3), (8, 3, 0, 2), (8, 3, 0, 0), (10, 1, 0, 1),
    (7, 3, 0, 2), (7, 2, 1, 0), (5, 3, 6), (7, 2, 0, 3), (10, 1, 0, 2), (8, 3, 0, 3), (5, 3, 7),
    (8, 3, 1, 2), (8, 2, 1, 3), (9, 0, 0, 3), (6, 1, 1, 1), (6, 0, 1, 1), (9, 3, 0, 3),
    (8, 3, 0, 1), (8, 2, 0, 2), (9, 0, 1, 2), (9, 3, 0, 2), (7, 3, 1, 2), (8, 3, 1, 3),
    (8, 3, 1, 0), (10, 0, 0, 3), (7, 3, 0, 1), (8, 2, 0, 3), (10, 1, 0, 3), (7, 3, 0, 0),
    (10, 0, 1, 2), (10, 3, 0, 3), (7, 2, 0, 1), (7, 2, 0, 2), (7, 3, 1, 0), (9, 0, 1, 0),
    (8, 2, 0, 0), (9, 3, 1, 2), (7, 3, 1, 3), (10, 3, 0, 2), (7, 2, 1, 2), (9, 3, 0, 1),
    (7, 2, 1, 3), (9, 3, 0, 0), (9, 1, 1, 2), (10, 0, 1, 3), (9, 2, 0, 1), (9, 2, 0, 2),
    (10, 3, 1, 2), (8, 0, 0, 0), (8, 3, 1, 1), (7, 3, 1, 1), (10, 0, 1, 1), (10, 1, 0, 0),
    (9, 3, 1, 3), (10, 3, 0, 1), (8, 2, 1, 1), (11, 1, 0), (10, 0, 0, 1), (7, 2, 1, 1),
    (9, 2, 1, 2), (10, 2, 0, 2), (9, 3, 1, 1), (9, 2, 0, 3), (10, 3, 0, 0), (7, 2, 0, 0),
    (9, 2, 1, 3), (9, 1, 1, 1), (8, 1, 1, 1), (10, 0, 0, 0), (10, 0, 1, 0), (11, 3, 0),
    (10, 3, 1, 3), (10, 2, 1, 2), (9, 2, 1, 1), (9, 3, 1, 0), (10, 1, 1, 2), (11, 0, 1),
    (10, 2, 0, 3), (10, 3, 1, 1), (11, 0, 0), (8, 2, 1, 0), (8, 1, 1, 3), (9, 2, 0, 0),
    (9, 1, 1, 3), (9, 2, 1, 0), (10, 2, 0, 1), (10, 2, 1, 3), (10, 2, 1, 1), (9, 1, 1, 0),
    (10, 3, 1, 0), (10, 1, 1, 1), (8, 1, 1, 0), (11, 3, 1), (10, 2, 0, 0), (11, 2, 0),
    (10, 1, 1, 3), (10, 2, 1, 0), (11, 2, 1), (10, 1, 1, 0), (11, 1, 1),
)
EPS = 1e-05
MASKED = -1e30


def dot(a, b):
    return jnp.dot(a, b, preferred_element_type=F32)


def kernel(
    q_ref, k_ref, v_ref, span_ref, gain_ref, router_ref, routes_ref, prio_ref,
    gate_hbm, up_hbm, down_hbm,
    out_ref,
    kv, own_scores, heads, held, normed, sends, arrived, tokens, gate_w, up_w, down_w,
    gate_acc, up_acc, hidden, parts, landed, crossed, back, returned, blend_ref,
    kv_s, kv_r, hd_s, hd_r, ds_s, ds_r, ag_s, ag_r, rs_s, rs_r, ov_s, ov_r, rt_s, rt_r, w_sem,
):
    ctx = lax.axis_index("ctx")
    me = lax.axis_index("exp")
    y = lax.rem(ctx, 4)
    zh = lax.rem(lax.div(ctx, 4), 2)
    x = lax.div(ctx, 8)

    def ctx_at(xx, zz, yy):
        return (xx * 2 + zz) * 4 + yy

    def near(axis, sign):
        step = 1 if sign > 0 else 3
        if axis == "x":
            return (ctx_at(lax.rem(x + step, 4), zh, y), me)
        return (ctx_at(x, zh, lax.rem(y + step, 4)), me)

    other_ctx = ctx_at(x, 1 - zh, y)

    bits = [lax.rem(me, 2), lax.rem(lax.div(me, 2), 2), lax.div(me, 4)]

    def partner(d):
        flipped = [1 - bit if d >> n & 1 else bit for n, bit in enumerate(bits)]
        return flipped[0] + 2 * flipped[1] + 4 * flipped[2]

    def ring(far, d):
        return (other_ctx if far else ctx, partner(d))

    def after(steps):
        return (lax.rem(ctx + steps + CTX, CTX), me)

    def remote(src, dst, s, r, device):
        return pltpu.make_async_remote_copy(
            src_ref=src, dst_ref=dst, send_sem=s, recv_sem=r,
            device_id=device, device_id_type=MESH,
        )

    weight_copies = [
        pltpu.make_async_copy(gate_hbm.at[0], gate_w, w_sem.at[0]),
        pltpu.make_async_copy(up_hbm.at[0], up_w, w_sem.at[1]),
        pltpu.make_async_copy(down_hbm.at[0], down_w, w_sem.at[2]),
    ]

    barrier = pltpu.get_barrier_semaphore()
    greeted = [after(-1), after(-2)]
    greeted += [ring(0, d) for d in range(1, EXP)]
    greeted += [near(axis, sign) for axis in "xy" for sign in (1, -1)]
    greeted += [ring(1, d) for d in range(EXP)]
    for device in greeted:
        pl.semaphore_signal(barrier, inc=1, device_id=device, device_id_type=MESH)

    def span_base(block, half):
        return span_ref[block * 2 + half] * SPAN

    blocks = [lax.rem(ctx + CTX - 2, CTX), lax.rem(ctx + CTX - 1, CTX), ctx]
    lane = lax.broadcasted_iota(jnp.int32, (TOK, 3 * TOK), 1)
    sub = lax.broadcasted_iota(jnp.int32, (TOK, 3 * TOK), 0)
    key_pos = lax.rem(lane, SPAN)
    lane_span = lax.div(lane, SPAN)
    for n in range(6):
        key_pos = key_pos + jnp.where(lane_span == n, span_base(blocks[n // 2], n % 2), 0)
    query_pos = lax.rem(sub, SPAN) + jnp.where(
        sub < SPAN, span_base(ctx, 0), span_base(ctx, 1)
    )
    visible = key_pos <= query_pos

    lane_t = lax.rem(lax.broadcasted_iota(jnp.int32, (ROWS, 64), 1), ROWS)
    pick = lax.broadcasted_iota(jnp.int32, (ROWS, 64), 0) == lane_t
    first = lax.broadcasted_iota(jnp.int32, (ROWS, 64), 1) < ROWS
    lane_16 = lax.broadcasted_iota(jnp.int32, (ROWS, ROWS), 1)
    sub_16 = lax.broadcasted_iota(jnp.int32, (ROWS, ROWS), 0)
    lane_32 = lax.broadcasted_iota(jnp.int32, (ROWS, 32), 1)
    sub_32 = lax.broadcasted_iota(jnp.int32, (ROWS, 32), 0)
    routes = routes_ref[...].astype(F32)
    prio = prio_ref[...].astype(F32)
    e_col = [
        jnp.sum(jnp.where(lane_16 == sub_16, routes[k : k + 1, :], 0.0), axis=1, keepdims=True)
        for k in range(2)
    ]
    p_col = [
        jnp.sum(jnp.where(lane_32 == 2 * sub_32 + k, prio, 0.0), axis=1, keepdims=True)
        for k in range(2)
    ]
    e_row = [jnp.sum(jnp.where(pick, e, 0.0), axis=0, keepdims=True) for e in e_col]
    p_row = [jnp.sum(jnp.where(pick, p, 0.0), axis=0, keepdims=True) for p in p_col]
    slot_row, slot_col = [], []
    for k in range(2):
        rank_row = jnp.zeros((1, 64), F32)
        rank_col = jnp.zeros((ROWS, 1), F32)
        for n in range(2):
            rank_row += jnp.sum(
                jnp.where((e_col[n] == e_row[k]) & (p_col[n] < p_row[k]), 1.0, 0.0),
                axis=0, keepdims=True,
            )
            rank_col += jnp.sum(
                jnp.where((e_row[n] == e_col[k]) & (p_row[n] < p_col[k]) & first, 1.0, 0.0),
                axis=1, keepdims=True,
            )
        slot_row.append(jnp.where(rank_row < CAP, e_row[k] * CAP + rank_row, -1.0))
        slot_col.append(jnp.where(rank_col < CAP, e_col[k] * CAP + rank_col, -1.0))

    lane_64 = lax.broadcasted_iota(jnp.int32, (128, 64), 1)
    row_128 = lax.broadcasted_iota(jnp.int32, (128, 64), 0)
    row_expert = lax.bitwise_xor(lax.div(row_128, 16), jnp.full_like(row_128, me))
    row_slot = (row_expert * CAP + lax.rem(row_128, 4)).astype(F32)
    same_part = lax.rem(lax.div(row_128, 4), 4) == lax.div(lane_64, ROWS)
    dispatch = jnp.where(
        same_part & ((slot_row[0] == row_slot) | (slot_row[1] == row_slot)), 1.0, 0.0
    ).astype(BF)
    row_64 = lax.broadcasted_iota(jnp.int32, (64, 64), 0)
    col_64 = lax.broadcasted_iota(jnp.int32, (64, 64), 1)
    swapped = lax.rem(lax.div(row_64, 4), 4) * 16 + lax.div(row_64, 16) * 4 + lax.rem(row_64, 4)
    swap = jnp.where(col_64 == swapped, 1.0, 0.0).astype(BF)

    def score(h, block):
        return lax.dot_general(
            q_ref[:, h * HD : (h + 1) * HD], block, (((1,), (1,)), ((), ())),
            preferred_element_type=F32,
        )

    for h in range(HEADS_HERE):
        own_scores[h] = score(h, k_ref[...])
    pl.semaphore_wait(barrier, len(greeted))

    kv_copies = []
    for which, ref in enumerate((k_ref, v_ref)):
        for back_steps in (1, 2):
            slot = which * 2 + back_steps - 1
            copy = remote(ref, kv.at[slot], kv_s.at[slot], kv_r.at[slot], after(back_steps))
            copy.start()
            kv_copies.append(copy)
    for copy in weight_copies:
        copy.start()

    head_copies = []
    for group in range(GROUPS):
        weights, denominators = [], []
        for h in range(group * GROUP_HEADS, (group + 1) * GROUP_HEADS):
            if h == 0:
                kv_copies[0].wait_recv()
                kv_copies[1].wait_recv()
            scores = jnp.concatenate(
                [score(h, kv[1]), score(h, kv[0]), own_scores[h]], axis=1
            ) * HD ** (-0.5)
            scores = jnp.where(visible, scores, MASKED)
            highest = jnp.max(scores, axis=1, keepdims=True)
            weight = jnp.where(visible, jnp.exp(scores - highest), 0.0)
            denominators.append(jnp.sum(weight, axis=1, keepdims=True))
            weights.append(weight.astype(BF))
        if group == 0:
            kv_copies[2].wait_recv()
            kv_copies[3].wait_recv()
        for n in range(GROUP_HEADS):
            total = dot(weights[n][:, :TOK], kv[3])
            total += dot(weights[n][:, TOK : 2 * TOK], kv[2])
            total += dot(weights[n][:, 2 * TOK :], v_ref[...])
            head = (total / denominators[n]).astype(BF)
            heads[group, :, :, n * HD : (n + 1) * HD] = head.reshape(EXP, ROWS, HD)
        for d in range(1, EXP):
            copy = remote(
                heads.at[group, partner(d)], held.at[group, me],
                hd_s.at[group, d], hd_r.at[group, d], ring(0, d),
            )
            copy.start()
            head_copies.append(copy)
        held[group, me] = heads[group, me]

    for copy in head_copies:
        copy.wait_recv()
    square = jnp.zeros((ROWS, 1), F32)
    for e in range(EXP):
        for group in range(GROUPS):
            block = held[group, e].astype(F32)
            square += jnp.sum(block * block, axis=1, keepdims=True)
    inverse = lax.rsqrt(square * (1.0 / D) + EPS)
    gain = gain_ref[...].astype(F32)
    for n in range(D // HD):
        e, h = n // HEADS_HERE, n % HEADS_HERE
        first_lane = h % GROUP_HEADS * HD
        block = held[h // GROUP_HEADS, e, :, first_lane : first_lane + HD].astype(F32)
        block = block * inverse * gain[n : n + 1, :]
        part, column = n // 12, n % 12 * HD
        normed[part * ROWS : (part + 1) * ROWS, column : column + HD] = block.astype(BF)

    sends[...] = dot(dispatch, normed[...]).astype(BF).reshape(EXP, 16, WIDE)
    slot_copies = {}

    def send_slots(far):
        for d in range(EXP):
            if not far and not d:
                continue
            n = far * EXP + d
            copy = remote(sends.at[d], arrived.at[n], ds_s.at[n], ds_r.at[n], ring(far, d))
            copy.start()
            slot_copies[n] = copy

    send_slots(0)
    arrived[0] = sends[0]

    def make_blend():
        logits = jnp.zeros((ROWS, EXP), F32)
        for part in range(PARTS):
            logits += lax.dot_general(
                normed[part * ROWS : (part + 1) * ROWS, :],
                router_ref[:, part * WIDE : (part + 1) * WIDE],
                (((1,), (1,)), ((), ())), preferred_element_type=F32,
            )
        lane_8 = lax.broadcasted_iota(jnp.int32, (ROWS, EXP), 1).astype(F32)
        picked = [
            jnp.sum(jnp.where(lane_8 == e, logits, 0.0), axis=1, keepdims=True) for e in e_col
        ]
        shares = [
            1.0 / (1.0 + jnp.exp(picked[1] - picked[0])),
            1.0 / (1.0 + jnp.exp(picked[0] - picked[1])),
        ]
        lane_256 = lax.broadcasted_iota(jnp.int32, (64, 256), 1)
        row_b = lax.broadcasted_iota(jnp.int32, (64, 256), 0)
        lane_expert = lax.bitwise_xor(
            lax.rem(lax.div(lane_256, 16), EXP), jnp.full_like(lane_256, me)
        )
        lane_slot = (lane_expert * CAP + lax.rem(lane_256, 4)).astype(F32)
        blend = jnp.zeros((64, 256), F32)
        for k in range(2):
            slot_tall = jnp.concatenate([slot_col[k]] * PARTS, axis=0)
            share_tall = jnp.concatenate([shares[k]] * PARTS, axis=0)
            blend += jnp.where(slot_tall == lane_slot, share_tall, 0.0)
        blend_ref[...] = jnp.where(
            lax.div(row_b, ROWS) == lax.rem(lax.div(lane_256, 4), 4), blend, 0.0
        )

    axes = [("x", "y"), ("y", "x"), ("x", "y"), ("y", "x")]
    first_sign = [1, -1, -1, 1]

    def second_sign(a):
        return 1 if a < 2 else -1

    def at(a, b):
        return a * 4 + b

    copies = {}

    def gather_copy(k, slot):
        a, b = divmod(slot, 4)
        if b:
            axis = axes[k][1]
            if b == 2:
                sign = second_sign(a)
                src = at(a, 3 if sign > 0 else 1)
            else:
                sign = 1 if b == 3 else -1
                src = at(a, 0)
        else:
            axis = axes[k][0]
            if a == 2:
                sign = first_sign[k]
                src = at(3 if sign > 0 else 1, 0)
            else:
                sign = 1 if a == 3 else -1
                src = 0
        if k >= 2 and b == 2 and a in CROSSING:
            src_ref, device = tokens.at[k - 2, slot], (other_ctx, me)
        else:
            src_ref, device = tokens.at[k, src], near(axis, sign)
        return remote(src_ref, tokens.at[k, slot], ag_s.at[k, slot], ag_r.at[k, slot], device)

    def sum_copy(k, c, n):
        if n < 12:
            a, kind = divmod(n, 3)
            axis, sign = axes[k][1], second_sign(a)
            ahead, behind = (1, 3) if sign > 0 else (3, 1)
            src = at(a, (2, ahead, behind)[kind])
        else:
            kind, axis, sign = n - 12, axes[k][0], first_sign[k]
            ahead, behind = (1, 3) if sign > 0 else (3, 1)
            src = at((2, ahead, behind)[kind], 0)
        return remote(
            parts.at[k, c, src], landed.at[k, c, n], rs_s.at[k, c, n], rs_r.at[k, c, n],
            near(axis, -sign if kind == 2 else sign),
        )

    def over_copy(k, c, a):
        n = OVER.index(a)
        return remote(
            parts.at[k, c, at(a, 2)], crossed.at[k, c, n], ov_s.at[k, c, n], ov_r.at[k, c, n],
            (other_ctx, me),
        )

    makers = {"gather": gather_copy, "sum": sum_copy, "over": over_copy}
    waited = set()

    def copy_of(*key):
        if key not in copies:
            copies[key] = makers[key[0]](*key[1:])
        return copies[key]

    def arrival(*key):
        if key not in waited:
            waited.add(key)
            copy_of(*key).wait_recv()

    def take_slots(k):
        first_n = (k // 2) * EXP + (k % 2) * 4
        for n in range(first_n, first_n + 4):
            if n:
                slot_copies[n].wait_recv()
        rows = arrived[first_n : first_n + 4].reshape(64, WIDE)
        moved = dot(swap, rows).astype(BF)
        for part in range(PARTS):
            tokens[k, 0, :, part * WIDE : (part + 1) * WIDE] = moved[part * 16 : (part + 1) * 16]

    def own(k):
        take_slots(k)
        copy_of("gather", k, at(3, 0)).start()
        copy_of("gather", k, at(1, 0)).start()
        if k == 1:
            send_slots(1)
            make_blend()

    def spread(k, a):
        if a:
            arrival("gather", k, at(a, 0))
        copy_of("gather", k, at(a, 3)).start()
        copy_of("gather", k, at(a, 1)).start()

    def forward(k):
        arrival("gather", k, at(3 if first_sign[k] > 0 else 1, 0))
        copy_of("gather", k, at(2, 0)).start()

    def onward(k, a):
        arrival("gather", k, at(a, 3 if second_sign(a) > 0 else 1))
        copy_of("gather", k, at(a, 2)).start()

    def cross(k, a):
        arrival("gather", k - 2, at(a, 2))
        copy_of("gather", k, at(a, 2)).start()

    def ffn(k, n):
        if n == 0:
            for slot in range(1, 16):
                arrival("gather", k, slot)
            if k == 0:
                for copy in weight_copies:
                    copy.wait()
        if n < PARTS:
            columns = slice(n * WIDE, (n + 1) * WIDE)
            rows = tokens[k, :, :, columns].reshape(256, WIDE)
            gate = dot(rows, gate_w[columns, :])
            up = dot(rows, up_w[columns, :])
            if n:
                gate = gate_acc[...] + gate
                up = up_acc[...] + up
            if n == PARTS - 1:
                hidden[...] = (gate / (1.0 + jnp.exp(-gate)) * up).astype(BF)
            else:
                gate_acc[...] = gate
                up_acc[...] = up
        else:
            column = (n - PARTS) * WIDE
            first_column = column % HALF
            parts[k, column // HALF, :, :, first_column : first_column + WIDE] = (
                dot(hidden[...], down_w[:, column : column + WIDE])
                .astype(BF).reshape(16, 16, WIDE)
            )

    def add(k, c, slot, *ns):
        total = parts[k, c, slot].astype(F32)
        for n in ns:
            arrival("sum", k, c, n)
            total += landed[k, c, n].astype(F32)
        parts[k, c, slot] = total.astype(BF)

    def over(k, c, a):
        copy_of("over", k, c, a).start()

    def far(k, c, a):
        if k >= 2 and a in OVER:
            arrival("over", k - 2, c, a)
            total = parts[k, c, at(a, 2)].astype(F32)
            total += crossed[k - 2, c, OVER.index(a)].astype(F32)
            parts[k, c, at(a, 2)] = total.astype(BF)
        copy_of("sum", k, c, a * 3).start()

    def side(k, c, a):
        copy_of("sum", k, c, a * 3 + 2).start()

    def middle(k, c, a):
        if k >= 2 or a not in OVER:
            add(k, c, at(a, 1 if second_sign(a) > 0 else 3), a * 3)
        copy_of("sum", k, c, a * 3 + 1).start()

    def close(k, c, a):
        ahead = 1 if first_sign[k] > 0 else 3
        more = {2: (), ahead: (12,), 4 - ahead: (), 0: (13, 14)}[a]
        add(k, c, at(a, 0), a * 3 + 1, a * 3 + 2, *more)
        if a:
            copy_of("sum", k, c, {2: 12, ahead: 13, 4 - ahead: 14}[a]).start()

    rt = {}

    def give(k, c):
        rows = jnp.concatenate(
            [parts[k, c, 0, :, n * NARROW : (n + 1) * NARROW] for n in range(PARTS)], axis=0
        )
        back[k, c] = dot(swap, rows).astype(BF).reshape(4, 16, NARROW)
        for m in range(4):
            d = (k % 2) * 4 + m
            n = (k // 2) * EXP + d
            if n:
                copy = remote(
                    back.at[k, c, m], returned.at[c, n], rt_s.at[c, n], rt_r.at[c, n],
                    ring(k // 2, d),
                )
                copy.start()
                rt[c, n] = copy
            else:
                returned[c, 0] = back[k, c, m]

    steps = [own, spread, forward, onward, cross, ffn, over, far, side, middle, close, give]
    for which, *where in ORDER:
        steps[which](*where)

    high = blend_ref[...].astype(BF)
    low = (blend_ref[...] - high.astype(F32)).astype(BF)
    for c in range(HALVES):
        for n in range(1, 2 * EXP):
            rt[c, n].wait_recv()
        came = returned[c].reshape(256, NARROW)
        mixed = dot(high, came) + dot(low, came)
        for part in range(PARTS):
            e = c * PARTS + part
            for group in range(GROUPS):
                columns = slice(group * GROUP_COLS, (group + 1) * GROUP_COLS)
                block = mixed[part * ROWS : (part + 1) * ROWS, columns]
                first_column = e * COLS + group * GROUP_COLS
                out_ref[:, first_column : first_column + GROUP_COLS] = (
                    held[group, e].astype(F32) + block
                ).astype(BF)

    for copy in kv_copies + head_copies + list(slot_copies.values()) + list(rt.values()):
        copy.wait_send()
    for copy in copies.values():
        copy.wait_send()


def body(
    queries, keys, values, span_order, norm_gain, router_weight, routes, priority,
    w_gate, w_up, w_down,
):
    vmem = pl.BlockSpec(memory_space=pltpu.VMEM)
    smem = pl.BlockSpec(memory_space=pltpu.SMEM)
    hbm = pl.BlockSpec(memory_space=pl.ANY)
    dma = pltpu.SemaphoreType.DMA
    return pl.pallas_call(
        kernel,
        out_shape=jax.ShapeDtypeStruct((ROWS, D), BF),
        in_specs=[vmem, vmem, vmem, smem, vmem, vmem, vmem, vmem, hbm, hbm, hbm],
        out_specs=vmem,
        scratch_shapes=[
            pltpu.VMEM((4, TOK, HD), BF),
            pltpu.VMEM((HEADS_HERE, TOK, TOK), F32),
            pltpu.VMEM((GROUPS, EXP, ROWS, GROUP_COLS), BF),
            pltpu.VMEM((GROUPS, EXP, ROWS, GROUP_COLS), BF),
            pltpu.VMEM((64, WIDE), BF),
            pltpu.VMEM((EXP, 16, WIDE), BF),
            pltpu.VMEM((2 * EXP, 16, WIDE), BF),
            pltpu.VMEM((4, 16, 16, D), BF),
            pltpu.VMEM((D, HID), BF),
            pltpu.VMEM((D, HID), BF),
            pltpu.VMEM((HID, D), BF),
            pltpu.VMEM((256, HID), F32),
            pltpu.VMEM((256, HID), F32),
            pltpu.VMEM((256, HID), BF),
            pltpu.VMEM((4, HALVES, 16, 16, HALF), BF),
            pltpu.VMEM((4, HALVES, 15, 16, HALF), BF),
            pltpu.VMEM((2, HALVES, len(OVER), 16, HALF), BF),
            pltpu.VMEM((4, HALVES, 4, 16, NARROW), BF),
            pltpu.VMEM((HALVES, 2 * EXP, 16, NARROW), BF),
            pltpu.VMEM((64, 256), F32),
            dma((4,)), dma((4,)),
            dma((GROUPS, EXP)), dma((GROUPS, EXP)),
            dma((2 * EXP,)), dma((2 * EXP,)),
            dma((4, 16)), dma((4, 16)),
            dma((4, HALVES, 15)), dma((4, HALVES, 15)),
            dma((2, HALVES, len(OVER))), dma((2, HALVES, len(OVER))),
            dma((HALVES, 2 * EXP)), dma((HALVES, 2 * EXP)),
            dma((3,)),
        ],
        compiler_params=pltpu.CompilerParams(
            collective_id=0, has_side_effects=True, vmem_limit_bytes=60 * 1024 * 1024
        ),
    )(
        queries, keys, values, span_order, norm_gain.reshape(D // HD, HD),
        router_weight.T, routes.T, priority, w_gate, w_up, w_down,
    )


def solution(mesh):
    placed = (
        P("ctx", "exp"),
        P("ctx", "exp"),
        P("ctx", "exp"),
        P(),
        P(),
        P(),
        P(("ctx", "exp"), None),
        P(("ctx", "exp"), None),
        P("exp", None, "ctx"),
        P("exp", None, "ctx"),
        P("exp", "ctx", None),
    )
    return jax.shard_map(
        body, mesh=mesh, in_specs=placed, out_specs=P(("ctx", "exp"), None), check_vma=False
    )
```

```python
import jax
import jax.numpy as jnp
from jax import lax
from jax.experimental import pallas as pl
from jax.experimental.pallas import tpu as pltpu
from jax.sharding import PartitionSpec as P

MESH = pl.DeviceIdType.MESH
BF = jnp.bfloat16
F32 = jnp.float32

HD = 128
HEADS_HERE = 6
TOK = 128
ROWS = 16
SPAN = 64
D = 6144
COLS = 768
EXP = 8
CTX = 32
CAP = 4
PARTS = 4
WIDE = D // PARTS
HALVES = 2
HALF = D // HALVES
NARROW = HALF // PARTS
GROUPS = 2
GROUP_HEADS = HEADS_HERE // GROUPS
GROUP_COLS = GROUP_HEADS * HD
HID = 256
CROSSING = (0, 3)
OVER = (2, 1)
ORDER = (
    (0, 0), (1, 0, 0), (0, 1), (3, 0, 0), (1, 1, 0), (2, 0), (1, 0, 1), (1, 1, 1), (2, 1),
    (3, 1, 0), (1, 1, 3), (0, 2), (1, 0, 3), (0, 3), (4, 2, 0), (3, 0, 1), (1, 0, 2), (1, 1, 2),
    (3, 0, 3), (4, 3, 0), (2, 2), (3, 1, 1), (3, 0, 2), (3, 1, 3), (1, 3, 3), (2, 3), (1, 2, 2),
    (3, 1, 2), (1, 2, 1), (1, 3, 1), (4, 2, 3), (5, 0, 0), (5, 0, 1), (4, 3, 3), (1, 3, 2),
    (5, 0, 2), (5, 0, 3), (5, 0, 4), (1, 2, 3), (5, 0, 5), (5, 0, 6), (9, 0, 0, 2), (3, 2, 1),
    (1, 2, 0), (5, 0, 7), (5, 1, 0), (6, 0, 0, 1), (5, 1, 1), (3, 3, 1), (5, 1, 2), (5, 1, 3),
    (5, 1, 4), (5, 1, 5), (1, 3, 0), (8, 0, 1, 3), (7, 1, 0, 3), (8, 1, 0, 0), (8, 0, 0, 2),
    (3, 2, 2), (5, 1, 6), (7, 0, 1, 3), (5, 1, 7), (7, 1, 0, 0), (3, 3, 2), (7, 0, 0, 0),
    (9, 1, 0, 2), (8, 1, 1, 2), (7, 0, 0, 3), (8, 0, 0, 1), (8, 0, 1, 0), (8, 1, 0, 1),
    (6, 1, 0, 2), (9, 1, 0, 1), (8, 1, 0, 2), (8, 0, 1, 1), (9, 1, 0, 0), (7, 1, 1, 0), (5, 2, 0),
    (5, 2, 1), (9, 1, 0, 3), (9, 0, 0, 1), (8, 1, 0, 3), (8, 0, 1, 2), (5, 2, 2), (8, 0, 0, 3),
    (5, 2, 3), (6, 1, 0, 1), (5, 2, 4), (9, 0, 0, 0), (7, 0, 1, 0), (5, 2, 5), (9, 0, 1, 1),
    (7, 1, 1, 3), (5, 2, 6), (5, 2, 7), (5, 3, 0), (6, 1, 1, 2), (8, 2, 1, 2), (5, 3, 1),
    (9, 0, 1, 3), (10, 0, 0, 2), (5, 3, 2), (5, 3, 3), (5, 3, 4), (5, 3, 5), (6, 0, 0, 2),
    (8, 2, 0, 1), (6, 0, 1, 2), (7, 3, 0, 3), (8, 3, 0, 2), (8, 3, 0, 0), (10, 1, 0, 1),
    (7, 3, 0, 2), (7, 2, 1, 0), (5, 3, 6), (7, 2, 0, 3), (10, 1, 0, 2), (8, 3, 0, 3), (5, 3, 7),
    (8, 3, 1, 2), (8, 2, 1, 3), (9, 0, 0, 3), (6, 1, 1, 1), (6, 0, 1, 1), (9, 3, 0, 3),
    (8, 3, 0, 1), (8, 2, 0, 2), (9, 0, 1, 2), (9, 3, 0, 2), (7, 3, 1, 2), (8, 3, 1, 3),
    (8, 3, 1, 0), (10, 0, 0, 3), (7, 3, 0, 1), (8, 2, 0, 3), (10, 1, 0, 3), (7, 3, 0, 0),
    (10, 0, 1, 2), (10, 3, 0, 3), (7, 2, 0, 1), (7, 2, 0, 2), (7, 3, 1, 0), (9, 0, 1, 0),
    (8, 2, 0, 0), (9, 3, 1, 2), (7, 3, 1, 3), (10, 3, 0, 2), (7, 2, 1, 2), (9, 3, 0, 1),
    (7, 2, 1, 3), (9, 3, 0, 0), (9, 1, 1, 2), (10, 0, 1, 3), (9, 2, 0, 1), (9, 2, 0, 2),
    (10, 3, 1, 2), (8, 0, 0, 0), (8, 3, 1, 1), (7, 3, 1, 1), (10, 0, 1, 1), (10, 1, 0, 0),
    (9, 3, 1, 3), (10, 3, 0, 1), (8, 2, 1, 1), (11, 1, 0), (10, 0, 0, 1), (7, 2, 1, 1),
    (9, 2, 1, 2), (10, 2, 0, 2), (9, 3, 1, 1), (9, 2, 0, 3), (10, 3, 0, 0), (7, 2, 0, 0),
    (9, 2, 1, 3), (9, 1, 1, 1), (8, 1, 1, 1), (10, 0, 0, 0), (10, 0, 1, 0), (11, 3, 0),
    (10, 3, 1, 3), (10, 2, 1, 2), (9, 2, 1, 1), (9, 3, 1, 0), (10, 1, 1, 2), (11, 0, 1),
    (10, 2, 0, 3), (10, 3, 1, 1), (11, 0, 0), (8, 2, 1, 0), (8, 1, 1, 3), (9, 2, 0, 0),
    (9, 1, 1, 3), (9, 2, 1, 0), (10, 2, 0, 1), (10, 2, 1, 3), (10, 2, 1, 1), (9, 1, 1, 0),
    (10, 3, 1, 0), (10, 1, 1, 1), (8, 1, 1, 0), (11, 3, 1), (10, 2, 0, 0), (11, 2, 0),
    (10, 1, 1, 3), (10, 2, 1, 0), (11, 2, 1), (10, 1, 1, 0), (11, 1, 1),
)
EPS = 1e-05
MASKED = -1e30


def dot(a, b):
    return jnp.dot(a, b, preferred_element_type=F32)


def kernel(
    q_ref, k_ref, v_ref, span_ref, gain_ref, router_ref, routes_ref, prio_ref,
    gate_hbm, up_hbm, down_hbm,
    out_ref,
    kv, own_scores, heads, held, normed, sends, arrived, tokens, gate_w, up_w, down_w,
    gate_acc, up_acc, hidden, parts, landed, crossed, back, returned, blend_ref,
    kv_s, kv_r, hd_s, hd_r, ds_s, ds_r, ag_s, ag_r, rs_s, rs_r, ov_s, ov_r, rt_s, rt_r, w_sem,
):
    ctx = lax.axis_index("ctx")
    me = lax.axis_index("exp")
    y = lax.rem(ctx, 4)
    zh = lax.rem(lax.div(ctx, 4), 2)
    x = lax.div(ctx, 8)

    def ctx_at(xx, zz, yy):
        return (xx * 2 + zz) * 4 + yy

    def near(axis, sign):
        step = 1 if sign > 0 else 3
        if axis == "x":
            return (ctx_at(lax.rem(x + step, 4), zh, y), me)
        return (ctx_at(x, zh, lax.rem(y + step, 4)), me)

    other_ctx = ctx_at(x, 1 - zh, y)

    bits = [lax.rem(me, 2), lax.rem(lax.div(me, 2), 2), lax.div(me, 4)]

    def partner(d):
        flipped = [1 - bit if d >> n & 1 else bit for n, bit in enumerate(bits)]
        return flipped[0] + 2 * flipped[1] + 4 * flipped[2]

    def ring(far, d):
        return (other_ctx if far else ctx, partner(d))

    def after(steps):
        return (lax.rem(ctx + steps + CTX, CTX), me)

    def remote(src, dst, s, r, device):
        return pltpu.make_async_remote_copy(
            src_ref=src, dst_ref=dst, send_sem=s, recv_sem=r,
            device_id=device, device_id_type=MESH,
        )

    weight_copies = [
        pltpu.make_async_copy(gate_hbm.at[0], gate_w, w_sem.at[0]),
        pltpu.make_async_copy(up_hbm.at[0], up_w, w_sem.at[1]),
        pltpu.make_async_copy(down_hbm.at[0], down_w, w_sem.at[2]),
    ]

    barrier = pltpu.get_barrier_semaphore()
    greeted = [after(-1), after(-2)]
    greeted += [ring(0, d) for d in range(1, EXP)]
    greeted += [near(axis, sign) for axis in "xy" for sign in (1, -1)]
    greeted += [ring(1, d) for d in range(EXP)]
    for device in greeted:
        pl.semaphore_signal(barrier, inc=1, device_id=device, device_id_type=MESH)

    def span_base(block, half):
        return span_ref[block * 2 + half] * SPAN

    blocks = [lax.rem(ctx + CTX - 2, CTX), lax.rem(ctx + CTX - 1, CTX), ctx]
    lane = lax.broadcasted_iota(jnp.int32, (TOK, 3 * TOK), 1)
    sub = lax.broadcasted_iota(jnp.int32, (TOK, 3 * TOK), 0)
    key_pos = lax.rem(lane, SPAN)
    lane_span = lax.div(lane, SPAN)
    for n in range(6):
        key_pos = key_pos + jnp.where(lane_span == n, span_base(blocks[n // 2], n % 2), 0)
    query_pos = lax.rem(sub, SPAN) + jnp.where(
        sub < SPAN, span_base(ctx, 0), span_base(ctx, 1)
    )
    visible = key_pos <= query_pos

    lane_t = lax.rem(lax.broadcasted_iota(jnp.int32, (ROWS, 64), 1), ROWS)
    pick = lax.broadcasted_iota(jnp.int32, (ROWS, 64), 0) == lane_t
    first = lax.broadcasted_iota(jnp.int32, (ROWS, 64), 1) < ROWS
    lane_16 = lax.broadcasted_iota(jnp.int32, (ROWS, ROWS), 1)
    sub_16 = lax.broadcasted_iota(jnp.int32, (ROWS, ROWS), 0)
    lane_32 = lax.broadcasted_iota(jnp.int32, (ROWS, 32), 1)
    sub_32 = lax.broadcasted_iota(jnp.int32, (ROWS, 32), 0)
    routes = routes_ref[...].astype(F32)
    prio = prio_ref[...].astype(F32)
    e_col = [
        jnp.sum(jnp.where(lane_16 == sub_16, routes[k : k + 1, :], 0.0), axis=1, keepdims=True)
        for k in range(2)
    ]
    p_col = [
        jnp.sum(jnp.where(lane_32 == 2 * sub_32 + k, prio, 0.0), axis=1, keepdims=True)
        for k in range(2)
    ]
    e_row = [jnp.sum(jnp.where(pick, e, 0.0), axis=0, keepdims=True) for e in e_col]
    p_row = [jnp.sum(jnp.where(pick, p, 0.0), axis=0, keepdims=True) for p in p_col]
    slot_row, slot_col = [], []
    for k in range(2):
        rank_row = jnp.zeros((1, 64), F32)
        rank_col = jnp.zeros((ROWS, 1), F32)
        for n in range(2):
            rank_row += jnp.sum(
                jnp.where((e_col[n] == e_row[k]) & (p_col[n] < p_row[k]), 1.0, 0.0),
                axis=0, keepdims=True,
            )
            rank_col += jnp.sum(
                jnp.where((e_row[n] == e_col[k]) & (p_row[n] < p_col[k]) & first, 1.0, 0.0),
                axis=1, keepdims=True,
            )
        slot_row.append(jnp.where(rank_row < CAP, e_row[k] * CAP + rank_row, -1.0))
        slot_col.append(jnp.where(rank_col < CAP, e_col[k] * CAP + rank_col, -1.0))

    lane_64 = lax.broadcasted_iota(jnp.int32, (128, 64), 1)
    row_128 = lax.broadcasted_iota(jnp.int32, (128, 64), 0)
    row_expert = lax.bitwise_xor(lax.div(row_128, 16), jnp.full_like(row_128, me))
    row_slot = (row_expert * CAP + lax.rem(row_128, 4)).astype(F32)
    same_part = lax.rem(lax.div(row_128, 4), 4) == lax.div(lane_64, ROWS)
    dispatch = jnp.where(
        same_part & ((slot_row[0] == row_slot) | (slot_row[1] == row_slot)), 1.0, 0.0
    ).astype(BF)
    row_64 = lax.broadcasted_iota(jnp.int32, (64, 64), 0)
    col_64 = lax.broadcasted_iota(jnp.int32, (64, 64), 1)
    swapped = lax.rem(lax.div(row_64, 4), 4) * 16 + lax.div(row_64, 16) * 4 + lax.rem(row_64, 4)
    swap = jnp.where(col_64 == swapped, 1.0, 0.0).astype(BF)

    def score(h, block):
        return lax.dot_general(
            q_ref[:, h * HD : (h + 1) * HD], block, (((1,), (1,)), ((), ())),
            preferred_element_type=F32,
        )

    for h in range(HEADS_HERE):
        own_scores[h] = score(h, k_ref[...])
    pl.semaphore_wait(barrier, len(greeted))

    kv_copies = []
    for which, ref in enumerate((k_ref, v_ref)):
        for back_steps in (1, 2):
            slot = which * 2 + back_steps - 1
            copy = remote(ref, kv.at[slot], kv_s.at[slot], kv_r.at[slot], after(back_steps))
            copy.start()
            kv_copies.append(copy)
    for copy in weight_copies:
        copy.start()

    head_copies = []
    for group in range(GROUPS):
        weights, denominators = [], []
        for h in range(group * GROUP_HEADS, (group + 1) * GROUP_HEADS):
            if h == 0:
                kv_copies[0].wait_recv()
                kv_copies[1].wait_recv()
            scores = jnp.concatenate(
                [score(h, kv[1]), score(h, kv[0]), own_scores[h]], axis=1
            ) * HD ** (-0.5)
            scores = jnp.where(visible, scores, MASKED)
            highest = jnp.max(scores, axis=1, keepdims=True)
            weight = jnp.where(visible, jnp.exp(scores - highest), 0.0)
            denominators.append(jnp.sum(weight, axis=1, keepdims=True))
            weights.append(weight.astype(BF))
        if group == 0:
            kv_copies[2].wait_recv()
            kv_copies[3].wait_recv()
        for n in range(GROUP_HEADS):
            total = dot(weights[n][:, :TOK], kv[3])
            total += dot(weights[n][:, TOK : 2 * TOK], kv[2])
            total += dot(weights[n][:, 2 * TOK :], v_ref[...])
            head = (total / denominators[n]).astype(BF)
            heads[group, :, :, n * HD : (n + 1) * HD] = head.reshape(EXP, ROWS, HD)
        for d in range(1, EXP):
            copy = remote(
                heads.at[group, partner(d)], held.at[group, me],
                hd_s.at[group, d], hd_r.at[group, d], ring(0, d),
            )
            copy.start()
            head_copies.append(copy)
        held[group, me] = heads[group, me]

    for copy in head_copies:
        copy.wait_recv()
    square = jnp.zeros((ROWS, 1), F32)
    for e in range(EXP):
        for group in range(GROUPS):
            block = held[group, e].astype(F32)
            square += jnp.sum(block * block, axis=1, keepdims=True)
    inverse = lax.rsqrt(square * (1.0 / D) + EPS)
    gain = gain_ref[...].astype(F32)
    for n in range(D // HD):
        e, h = n // HEADS_HERE, n % HEADS_HERE
        first_lane = h % GROUP_HEADS * HD
        block = held[h // GROUP_HEADS, e, :, first_lane : first_lane + HD].astype(F32)
        block = block * inverse * gain[n : n + 1, :]
        part, column = n // 12, n % 12 * HD
        normed[part * ROWS : (part + 1) * ROWS, column : column + HD] = block.astype(BF)

    sends[...] = dot(dispatch, normed[...]).astype(BF).reshape(EXP, 16, WIDE)
    slot_copies = {}

    def send_slots(far):
        for d in range(EXP):
            if not far and not d:
                continue
            n = far * EXP + d
            copy = remote(sends.at[d], arrived.at[n], ds_s.at[n], ds_r.at[n], ring(far, d))
            copy.start()
            slot_copies[n] = copy

    send_slots(0)
    arrived[0] = sends[0]

    def make_blend():
        logits = jnp.zeros((ROWS, EXP), F32)
        for part in range(PARTS):
            logits += lax.dot_general(
                normed[part * ROWS : (part + 1) * ROWS, :],
                router_ref[:, part * WIDE : (part + 1) * WIDE],
                (((1,), (1,)), ((), ())), preferred_element_type=F32,
            )
        lane_8 = lax.broadcasted_iota(jnp.int32, (ROWS, EXP), 1).astype(F32)
        picked = [
            jnp.sum(jnp.where(lane_8 == e, logits, 0.0), axis=1, keepdims=True) for e in e_col
        ]
        shares = [
            1.0 / (1.0 + jnp.exp(picked[1] - picked[0])),
            1.0 / (1.0 + jnp.exp(picked[0] - picked[1])),
        ]
        lane_256 = lax.broadcasted_iota(jnp.int32, (64, 256), 1)
        row_b = lax.broadcasted_iota(jnp.int32, (64, 256), 0)
        lane_expert = lax.bitwise_xor(
            lax.rem(lax.div(lane_256, 16), EXP), jnp.full_like(lane_256, me)
        )
        lane_slot = (lane_expert * CAP + lax.rem(lane_256, 4)).astype(F32)
        blend = jnp.zeros((64, 256), F32)
        for k in range(2):
            slot_tall = jnp.concatenate([slot_col[k]] * PARTS, axis=0)
            share_tall = jnp.concatenate([shares[k]] * PARTS, axis=0)
            blend += jnp.where(slot_tall == lane_slot, share_tall, 0.0)
        blend_ref[...] = jnp.where(
            lax.div(row_b, ROWS) == lax.rem(lax.div(lane_256, 4), 4), blend, 0.0
        )

    axes = [("x", "y"), ("y", "x"), ("x", "y"), ("y", "x")]
    first_sign = [1, -1, -1, 1]

    def second_sign(a):
        return 1 if a < 2 else -1

    def at(a, b):
        return a * 4 + b

    copies = {}

    def gather_copy(k, slot):
        a, b = divmod(slot, 4)
        if b:
            axis = axes[k][1]
            if b == 2:
                sign = second_sign(a)
                src = at(a, 3 if sign > 0 else 1)
            else:
                sign = 1 if b == 3 else -1
                src = at(a, 0)
        else:
            axis = axes[k][0]
            if a == 2:
                sign = first_sign[k]
                src = at(3 if sign > 0 else 1, 0)
            else:
                sign = 1 if a == 3 else -1
                src = 0
        if k >= 2 and b == 2 and a in CROSSING:
            src_ref, device = tokens.at[k - 2, slot], (other_ctx, me)
        else:
            src_ref, device = tokens.at[k, src], near(axis, sign)
        return remote(src_ref, tokens.at[k, slot], ag_s.at[k, slot], ag_r.at[k, slot], device)

    def sum_copy(k, c, n):
        if n < 12:
            a, kind = divmod(n, 3)
            axis, sign = axes[k][1], second_sign(a)
            ahead, behind = (1, 3) if sign > 0 else (3, 1)
            src = at(a, (2, ahead, behind)[kind])
        else:
            kind, axis, sign = n - 12, axes[k][0], first_sign[k]
            ahead, behind = (1, 3) if sign > 0 else (3, 1)
            src = at((2, ahead, behind)[kind], 0)
        return remote(
            parts.at[k, c, src], landed.at[k, c, n], rs_s.at[k, c, n], rs_r.at[k, c, n],
            near(axis, -sign if kind == 2 else sign),
        )

    def over_copy(k, c, a):
        n = OVER.index(a)
        return remote(
            parts.at[k, c, at(a, 2)], crossed.at[k, c, n], ov_s.at[k, c, n], ov_r.at[k, c, n],
            (other_ctx, me),
        )

    makers = {"gather": gather_copy, "sum": sum_copy, "over": over_copy}
    waited = set()

    def copy_of(*key):
        if key not in copies:
            copies[key] = makers[key[0]](*key[1:])
        return copies[key]

    def arrival(*key):
        if key not in waited:
            waited.add(key)
            copy_of(*key).wait_recv()

    def take_slots(k):
        first_n = (k // 2) * EXP + (k % 2) * 4
        for n in range(first_n, first_n + 4):
            if n:
                slot_copies[n].wait_recv()
        rows = arrived[first_n : first_n + 4].reshape(64, WIDE)
        moved = dot(swap, rows).astype(BF)
        for part in range(PARTS):
            tokens[k, 0, :, part * WIDE : (part + 1) * WIDE] = moved[part * 16 : (part + 1) * 16]

    def own(k):
        take_slots(k)
        copy_of("gather", k, at(3, 0)).start()
        copy_of("gather", k, at(1, 0)).start()
        if k == 0:
            send_slots(1)
        if k == 1:
            make_blend()

    def spread(k, a):
        if a:
            arrival("gather", k, at(a, 0))
        copy_of("gather", k, at(a, 3)).start()
        copy_of("gather", k, at(a, 1)).start()

    def forward(k):
        arrival("gather", k, at(3 if first_sign[k] > 0 else 1, 0))
        copy_of("gather", k, at(2, 0)).start()

    def onward(k, a):
        arrival("gather", k, at(a, 3 if second_sign(a) > 0 else 1))
        copy_of("gather", k, at(a, 2)).start()

    def cross(k, a):
        arrival("gather", k - 2, at(a, 2))
        copy_of("gather", k, at(a, 2)).start()

    def ffn(k, n):
        if n == 0:
            for slot in range(1, 16):
                arrival("gather", k, slot)
            if k == 0:
                for copy in weight_copies:
                    copy.wait()
        if n < PARTS:
            columns = slice(n * WIDE, (n + 1) * WIDE)
            rows = tokens[k, :, :, columns].reshape(256, WIDE)
            gate = dot(rows, gate_w[columns, :])
            up = dot(rows, up_w[columns, :])
            if n:
                gate = gate_acc[...] + gate
                up = up_acc[...] + up
            if n == PARTS - 1:
                hidden[...] = (gate / (1.0 + jnp.exp(-gate)) * up).astype(BF)
            else:
                gate_acc[...] = gate
                up_acc[...] = up
        else:
            column = (n - PARTS) * WIDE
            first_column = column % HALF
            parts[k, column // HALF, :, :, first_column : first_column + WIDE] = (
                dot(hidden[...], down_w[:, column : column + WIDE])
                .astype(BF).reshape(16, 16, WIDE)
            )

    def add(k, c, slot, *ns):
        total = parts[k, c, slot].astype(F32)
        for n in ns:
            arrival("sum", k, c, n)
            total += landed[k, c, n].astype(F32)
        parts[k, c, slot] = total.astype(BF)

    def over(k, c, a):
        copy_of("over", k, c, a).start()

    def far(k, c, a):
        if k >= 2 and a in OVER:
            arrival("over", k - 2, c, a)
            total = parts[k, c, at(a, 2)].astype(F32)
            total += crossed[k - 2, c, OVER.index(a)].astype(F32)
            parts[k, c, at(a, 2)] = total.astype(BF)
        copy_of("sum", k, c, a * 3).start()

    def side(k, c, a):
        copy_of("sum", k, c, a * 3 + 2).start()

    def middle(k, c, a):
        if k >= 2 or a not in OVER:
            add(k, c, at(a, 1 if second_sign(a) > 0 else 3), a * 3)
        copy_of("sum", k, c, a * 3 + 1).start()

    def close(k, c, a):
        ahead = 1 if first_sign[k] > 0 else 3
        more = {2: (), ahead: (12,), 4 - ahead: (), 0: (13, 14)}[a]
        add(k, c, at(a, 0), a * 3 + 1, a * 3 + 2, *more)
        if a:
            copy_of("sum", k, c, {2: 12, ahead: 13, 4 - ahead: 14}[a]).start()

    rt = {}

    def give(k, c):
        rows = jnp.concatenate(
            [parts[k, c, 0, :, n * NARROW : (n + 1) * NARROW] for n in range(PARTS)], axis=0
        )
        back[k, c] = dot(swap, rows).astype(BF).reshape(4, 16, NARROW)
        for m in range(4):
            d = (k % 2) * 4 + m
            n = (k // 2) * EXP + d
            if n:
                copy = remote(
                    back.at[k, c, m], returned.at[c, n], rt_s.at[c, n], rt_r.at[c, n],
                    ring(k // 2, d),
                )
                copy.start()
                rt[c, n] = copy
            else:
                returned[c, 0] = back[k, c, m]

    steps = [own, spread, forward, onward, cross, ffn, over, far, side, middle, close, give]
    for which, *where in ORDER:
        steps[which](*where)

    high = blend_ref[...].astype(BF)
    low = (blend_ref[...] - high.astype(F32)).astype(BF)
    for c in range(HALVES):
        for n in range(1, 2 * EXP):
            rt[c, n].wait_recv()
        came = returned[c].reshape(256, NARROW)
        mixed = dot(high, came) + dot(low, came)
        for part in range(PARTS):
            e = c * PARTS + part
            for group in range(GROUPS):
                columns = slice(group * GROUP_COLS, (group + 1) * GROUP_COLS)
                block = mixed[part * ROWS : (part + 1) * ROWS, columns]
                first_column = e * COLS + group * GROUP_COLS
                out_ref[:, first_column : first_column + GROUP_COLS] = (
                    held[group, e].astype(F32) + block
                ).astype(BF)

    for copy in kv_copies + head_copies + list(slot_copies.values()) + list(rt.values()):
        copy.wait_send()
    for copy in copies.values():
        copy.wait_send()


def body(
    queries, keys, values, span_order, norm_gain, router_weight, routes, priority,
    w_gate, w_up, w_down,
):
    vmem = pl.BlockSpec(memory_space=pltpu.VMEM)
    smem = pl.BlockSpec(memory_space=pltpu.SMEM)
    hbm = pl.BlockSpec(memory_space=pl.ANY)
    dma = pltpu.SemaphoreType.DMA
    return pl.pallas_call(
        kernel,
        out_shape=jax.ShapeDtypeStruct((ROWS, D), BF),
        in_specs=[vmem, vmem, vmem, smem, vmem, vmem, vmem, vmem, hbm, hbm, hbm],
        out_specs=vmem,
        scratch_shapes=[
            pltpu.VMEM((4, TOK, HD), BF),
            pltpu.VMEM((HEADS_HERE, TOK, TOK), F32),
            pltpu.VMEM((GROUPS, EXP, ROWS, GROUP_COLS), BF),
            pltpu.VMEM((GROUPS, EXP, ROWS, GROUP_COLS), BF),
            pltpu.VMEM((64, WIDE), BF),
            pltpu.VMEM((EXP, 16, WIDE), BF),
            pltpu.VMEM((2 * EXP, 16, WIDE), BF),
            pltpu.VMEM((4, 16, 16, D), BF),
            pltpu.VMEM((D, HID), BF),
            pltpu.VMEM((D, HID), BF),
            pltpu.VMEM((HID, D), BF),
            pltpu.VMEM((256, HID), F32),
            pltpu.VMEM((256, HID), F32),
            pltpu.VMEM((256, HID), BF),
            pltpu.VMEM((4, HALVES, 16, 16, HALF), BF),
            pltpu.VMEM((4, HALVES, 15, 16, HALF), BF),
            pltpu.VMEM((2, HALVES, len(OVER), 16, HALF), BF),
            pltpu.VMEM((4, HALVES, 4, 16, NARROW), BF),
            pltpu.VMEM((HALVES, 2 * EXP, 16, NARROW), BF),
            pltpu.VMEM((64, 256), F32),
            dma((4,)), dma((4,)),
            dma((GROUPS, EXP)), dma((GROUPS, EXP)),
            dma((2 * EXP,)), dma((2 * EXP,)),
            dma((4, 16)), dma((4, 16)),
            dma((4, HALVES, 15)), dma((4, HALVES, 15)),
            dma((2, HALVES, len(OVER))), dma((2, HALVES, len(OVER))),
            dma((HALVES, 2 * EXP)), dma((HALVES, 2 * EXP)),
            dma((3,)),
        ],
        compiler_params=pltpu.CompilerParams(
            collective_id=0, has_side_effects=True, vmem_limit_bytes=60 * 1024 * 1024
        ),
    )(
        queries, keys, values, span_order, norm_gain.reshape(D // HD, HD),
        router_weight.T, routes.T, priority, w_gate, w_up, w_down,
    )


def solution(mesh):
    placed = (
        P("ctx", "exp"),
        P("ctx", "exp"),
        P("ctx", "exp"),
        P(),
        P(),
        P(),
        P(("ctx", "exp"), None),
        P(("ctx", "exp"), None),
        P("exp", None, "ctx"),
        P("exp", None, "ctx"),
        P("exp", "ctx", None),
    )
    return jax.shard_map(
        body, mesh=mesh, in_specs=placed, out_specs=P(("ctx", "exp"), None), check_vma=False
    )
```
